1024 devices in a mesh: zone: 64 (over z, core), level: 16 (over x, y).
Axes of the slice: x: 4, y: 4, z: 32, core: 2. Of those that a mesh axis runs over, the one named last changes fastest.
Arguments:
- multipoles: bfloat16 [16384, 121], P(('zone', 'level')), may hold values from -6 to 6
- operators: bfloat16 [189, 121, 121], replicated, may hold values from -0.0390625 to 0.0390625
- parent_locals: float32 [2048, 121], P(('zone', 'level')), may hold values from -6 to 6
- shifts: float32 [8, 121, 121], replicated, may hold values from -0.5 to 0.5
- send_slots: int32 [1024, 64, 4], P(('zone', 'level')), may hold values from -1 to 15, as said below
- lists: int32 [16384, 189], P(('zone', 'level')), may hold values from -1 to 271, as said below
- positions: float32 [16384, 3, 256], P(('zone', 'level')), may hold values from 0 to 544, as said below
- charges: float32 [16384, 256], P(('zone', 'level')), may hold values from -0.09 to 0.09
- counts: int32 [16384], P(('zone', 'level')), may hold values from 64 to 256
- near_lists: int32 [16384, 27], P(('zone', 'level')), may hold values from -1 to 47, as said below
Outputs:
- local_coeffs: float32 [16384, 121], P(('zone', 'level'))
- potential: float32 [16384, 256], P(('zone', 'level'))
The draws below stay inside these ranges and needn't reach their ends.
Inputs may be any that keep to these rules, and one draw needn't show every extreme that they name: `send_slots`: A tile's non-empty slots toward a reader zone come first; each tile fills all 4 slots toward some zones and 1 to 4 toward others. `lists`: an entry of 16 or more always names a non-empty slot. `near_lists`: the first entry of each box names the box itself; the others name, in an order drawn for each box, some of the boxes whose cubes touch its cube among the same zone's groups l - 1, l, l + 1 (which ones is drawn), and -1 elsewhere; box n is in the list of box b exactly when b is in the list of n. `positions`: each box's particles lie in its own cube of side 0.5; a group's boxes form one layer of cubes in Morton order, a zone's groups are stacked layers.
All inputs are finite; a program needn't handle non-finite values.
Results may differ from the reference program's by a relative error of at most 0.0003.
Values may be sent and summed in bfloat16 or wider, within the bound.
A program may use at most 32 MiB of HBM per device.

```python
import jax
import jax.numpy as jnp
from jax import lax

BOX_DEV = 16
CAP = 4
S = 256
OFFSETS = 189
NEAR = 27
CHILDREN = 8
P2 = 121
ZONES = 64
LEVELS = 16
BOXES = 16384


def slot_counts(key):
    groups = ZONES * LEVELS
    drawn = jax.random.randint(key, (groups, ZONES), 1, CAP + 1)
    sender_zone = jnp.arange(groups, dtype=jnp.int32)[:, None] // LEVELS
    reader_zone = jnp.arange(ZONES, dtype=jnp.int32)[None, :]
    return jnp.where((sender_zone + reader_zone) % 3 == 0, CAP, drawn).astype(jnp.int32)


def box_place(local_index):
    bit_total = BOX_DEV.bit_length() - 1
    across = jnp.zeros_like(local_index)
    along = jnp.zeros_like(local_index)
    for place in range(bit_total):
        digit = local_index // 2 ** place % 2
        if place % 2 == 0:
            across = across + digit * 2 ** (place // 2)
        else:
            along = along + digit * 2 ** (place // 2)
    return (across, along)


def box_code(across, along):
    bit_total = BOX_DEV.bit_length() - 1
    code = jnp.zeros_like(across)
    for place in range(bit_total):
        if place % 2 == 0:
            code = code + across // 2 ** (place // 2) % 2 * 2 ** place
        else:
            code = code + along // 2 ** (place // 2) % 2 * 2 ** place
    return code


def draw_send_slots(key, part):
    filled = slot_counts(key)
    key = jax.random.fold_in(key, 11)
    boxes_drawn = jax.random.randint(key, (ZONES * LEVELS, ZONES, CAP), 0, BOX_DEV)
    slot_index = jnp.arange(CAP, dtype=jnp.int32)[None, None, :]
    return jnp.where(slot_index < filled[:, :, None], boxes_drawn, -1).astype(jnp.int32)


def draw_lists(key, part):
    filled = slot_counts(key)
    key = jax.random.fold_in(key, 12)
    key_kind, key_local, key_peer, key_slot = jax.random.split(key, 4)
    box_index = jnp.arange(BOXES, dtype=jnp.int32)[:, None]
    group_index = box_index // BOX_DEV
    zone_index = group_index // LEVELS
    level_index = group_index % LEVELS
    kind_draw = jax.random.randint(key_kind, (BOXES, OFFSETS), 0, 10)
    local_draw = jax.random.randint(key_local, (BOXES, OFFSETS), 0, BOX_DEV)
    peer_zone = jax.random.randint(key_peer, (BOXES, OFFSETS), 0, ZONES)
    slot_draw = jax.random.randint(key_slot, (BOXES, OFFSETS), 0, 1 << 20)
    sender = peer_zone * LEVELS + level_index
    count_here = filled[sender, zone_index]
    remote_entry = BOX_DEV + peer_zone * CAP + slot_draw % count_here
    entries = jnp.where(kind_draw < 2, -1, jnp.where(kind_draw < 4, local_draw, remote_entry))
    return entries.astype(jnp.int32)


def draw_near_lists(key, part):
    key = jax.random.fold_in(key, 13)
    key_order, key_keep = jax.random.split(key, 2)
    bit_total = BOX_DEV.bit_length() - 1
    width_across = 2 ** ((bit_total + 1) // 2)
    width_along = 2 ** (bit_total // 2)
    box_index = jnp.arange(BOXES, dtype=jnp.int32)
    group_index = box_index // BOX_DEV
    level_index = group_index % LEVELS
    local_index = box_index % BOX_DEV
    across, along = box_place(local_index)
    tags = jax.random.randint(key_keep, (BOXES,), 0, 4)
    columns = []
    for step_level in (-1, 0, 1):
        for step_across in (-1, 0, 1):
            for step_along in (-1, 0, 1):
                if step_level == 0 and step_across == 0 and (step_along == 0):
                    continue
                next_across = across + step_across
                next_along = along + step_along
                next_level = level_index + step_level
                valid = (next_across >= 0) & (next_across < width_across) & (next_along >= 0) & (next_along < width_along) & (next_level >= 0) & (next_level < LEVELS)
                code = box_code(jnp.clip(next_across, 0, width_across - 1), jnp.clip(next_along, 0, width_along - 1))
                neighbour = jnp.clip((group_index + step_level) * BOX_DEV + code, 0, BOXES - 1)
                kept = (tags + tags[neighbour]) % 4 != 0
                columns.append(jnp.where(valid & kept, (step_level + 1) * BOX_DEV + code, -1))
    others = jnp.stack(columns, axis=1)
    scores = jax.random.randint(key_order, (BOXES, NEAR - 1), 0, 1 << 16) * 32 + jnp.arange(NEAR - 1, dtype=jnp.int32)[None, :]
    order = jnp.argsort(scores, axis=1, stable=True)
    others = jnp.take_along_axis(others, order, axis=1)
    own_entry = (local_index + BOX_DEV)[:, None]
    return jnp.concatenate([own_entry, others], axis=1).astype(jnp.int32)


def draw_positions(key, part):
    key = jax.random.fold_in(key, 15)
    box_index = jnp.arange(BOXES, dtype=jnp.int32)
    group_index = box_index // BOX_DEV
    zone_index = group_index // LEVELS
    level_index = group_index % LEVELS
    across, along = box_place(box_index % BOX_DEV)
    height = zone_index * (LEVELS + 1) + level_index
    corner = jnp.stack([across, along, height], axis=1).astype(jnp.float32)
    jitter = jax.random.uniform(key, (BOXES, 3, S), jnp.float32, 0.0, 1.0)
    return ((corner[:, :, None] + jitter) * 0.5).astype(jnp.float32)


def draw_counts(key, part):
    key = jax.random.fold_in(key, 14)
    key_count, key_full = jax.random.split(key, 2)
    drawn = jax.random.randint(key_count, (BOXES,), S // 4, S + 1)
    full_draw = jax.random.randint(key_full, (BOXES,), 0, 5) == 0
    box_index = jnp.arange(BOXES, dtype=jnp.int32)
    return jnp.where(full_draw | (box_index == 0), S, drawn).astype(jnp.int32)


def levels(stream_key, dims, pieces, low, high):
    def one(position, parts):
        heights = jax.random.uniform(jax.random.fold_in(jax.random.fold_in(stream_key, 6), position), (parts,), jnp.float32, low / len(pieces), high / len(pieces))
        return jnp.repeat(jnp.exp(heights), dims[position] // parts).reshape((-1,) + (1,) * (len(dims) - position - 1))

    loudness = one(*pieces[0])
    for cut in pieces[1:]:
        loudness = loudness * one(*cut)
    return loudness


def normal_values(key, extent, scale, bound, shards=(), kind=jnp.bfloat16):
    values = scale * jax.random.normal(key, extent, jnp.float32)
    if shards:
        values = values * levels(key, extent, shards, -0.22, 0.18)
    return jnp.clip(values, -bound, bound).astype(kind)


def setup_inputs(seed: int = 0) -> dict:
    key_of = jax.random.split(jax.random.key(seed), 11)
    return {
        "multipoles": normal_values(key_of[0], (BOXES, P2), 1.0, 6.0, ((0, 1024),)),
        "operators": normal_values(key_of[1], (OFFSETS, P2, P2), (P2 * OFFSETS) ** -0.5, 0.0390625),
        "parent_locals": normal_values(key_of[2], (BOXES // CHILDREN, P2), 1.0, 6.0, ((0, 1024),), jnp.float32),
        "shifts": normal_values(key_of[3], (CHILDREN, P2, P2), P2 ** -0.5, 0.5, (), jnp.float32),
        "send_slots": draw_send_slots(jax.random.fold_in(key_of[10], 71), 0),
        "lists": draw_lists(jax.random.fold_in(key_of[10], 71), 0),
        "positions": draw_positions(jax.random.fold_in(key_of[10], 71), 0),
        "charges": normal_values(key_of[7], (BOXES, S), 0.015, 0.09, ((0, 1024),), jnp.float32),
        "counts": draw_counts(jax.random.fold_in(key_of[10], 71), 0),
        "near_lists": draw_near_lists(jax.random.fold_in(key_of[10], 71), 0),
    }


soften = 0.0025

def near_field(window, near_rows, occupied_rows, box_dev):
    slot_count = window.shape[2]
    targets = window[box_dev:2 * box_dev]
    own_index = jnp.arange(box_dev, dtype=jnp.int32) + box_dev
    diagonal = jnp.arange(slot_count)[:, None] == jnp.arange(slot_count)[None, :]

    def one_member(column, running):
        list_entry = near_rows[:, column]
        present = list_entry >= 0
        sources = window[jnp.maximum(list_entry, 0)]
        distance = soften
        for component in range(3):
            offset = targets[:, component, :, None] - sources[:, component, None, :]
            distance = distance + offset * offset
        kernel = lax.rsqrt(distance)
        self_pair = (list_entry == own_index)[:, None, None] & diagonal[None]
        kernel = jnp.where(self_pair, 0.0, kernel)
        partial_sum = lax.optimization_barrier(jnp.sum(kernel * sources[:, 3, None, :], axis=2))
        return running + jnp.where(present[:, None], partial_sum, 0.0)
    running = lax.fori_loop(0, near_rows.shape[1], one_member, jnp.zeros((box_dev, slot_count), jnp.float32))
    return jnp.where(occupied_rows, running, 0.0)

def reference(multipoles, operators, parent_locals, shifts, send_slots, lists, positions, charges, counts, near_lists):
    groups = ZONES * LEVELS
    slot_rows = jnp.arange(S, dtype=jnp.int32)
    occupied = slot_rows[None, :] < counts[:, None]
    charged = jnp.where(occupied, charges, 0.0)
    packed = jnp.concatenate([positions, charged[:, None, :]], axis=1)
    padding = jnp.zeros((BOX_DEV, 4, S), packed.dtype)
    padded = jnp.concatenate([padding, packed, padding], axis=0)
    flat_ops = operators.reshape(OFFSETS * P2, P2)
    downward = jnp.einsum('gp,cpq->gcq', parent_locals, shifts, precision=lax.Precision.HIGHEST).reshape(BOXES, P2)

    def per_group(group_index):
        first_row = (group_index * BOX_DEV).astype(jnp.int32)
        window = lax.dynamic_slice_in_dim(padded, first_row, 3 * BOX_DEV, 0)
        near_rows = lax.dynamic_slice_in_dim(near_lists, first_row, BOX_DEV, 0)
        occupied_rows = lax.dynamic_slice_in_dim(occupied, first_row, BOX_DEV, 0)
        potential_rows = near_field(window, near_rows, occupied_rows, BOX_DEV)
        entries = lax.dynamic_slice_in_dim(lists, first_row, BOX_DEV, 0)
        zone_index = group_index // LEVELS
        level_index = group_index % LEVELS
        remote = jnp.maximum(entries - BOX_DEV, 0)
        peer_zone = remote // CAP
        slot_index = remote % CAP
        sender = peer_zone * LEVELS + level_index
        remote_box = send_slots[sender, zone_index, slot_index]
        row_index = jnp.where(entries < BOX_DEV, first_row + entries, sender * BOX_DEV + remote_box)
        present = entries >= 0
        row_index = jnp.where(present, row_index, 0).astype(jnp.int32)
        gathered = multipoles[row_index]
        gathered = jnp.where(present[:, :, None], gathered, jnp.zeros((), gathered.dtype))
        far_field = jnp.dot(gathered.reshape(BOX_DEV, OFFSETS * P2), flat_ops, preferred_element_type=jnp.float32)
        return (far_field, potential_rows)
    far_all, potential_all = lax.map(per_group, jnp.arange(groups, dtype=jnp.int32))
    local_coeffs = far_all.reshape(BOXES, P2) + downward
    return (local_coeffs, potential_all.reshape(BOXES, S))
```

```python
import jax
import jax.numpy as jnp
from jax import lax
from jax.experimental import pallas as pl
from jax.experimental.pallas import tpu as pltpu
from jax.sharding import PartitionSpec as P

soften = 0.0025
BOX = 16
S = 256
HALF = 128
FEATURES = 32
NEAR = 27
WINDOW = 48
OFFSETS = 189
P2 = 121
GROUP = 8
ROWS = 32
TABLE = 384
MESH = pl.DeviceIdType.MESH
F32 = jnp.float32
BF16 = jnp.bfloat16


def iota(shape, dim):
    return lax.broadcasted_iota(jnp.int32, shape, dim)


def flag(mask, kind=BF16):
    return jnp.where(mask, 1.0, 0.0).astype(kind)


def dot(a, b):
    return jnp.dot(a, b, preferred_element_type=F32)


def dot_t(a, b):
    return lax.dot_general(a, b, (((1,), (1,)), ((), ())), preferred_element_type=F32)


def code(across, along):
    return across % 2 + 4 * (across // 2) + 2 * (along % 2) + 8 * (along // 2)


def split(x):
    high = x.astype(BF16).astype(F32)
    rest = x - high
    middle = rest.astype(BF16).astype(F32)
    return high, middle, rest - middle


def write_features(ref, coordinates, target):
    parts = [split(u) for u in coordinates]
    norm = coordinates[0] * coordinates[0]
    for u in coordinates[1:]:
        norm = norm + u * u
    ones = jnp.ones_like(norm)
    zeros = jnp.zeros_like(norm)
    rows = []
    for high, middle, low in parts:
        if target:
            rows += [-2.0 * r for r in (high, high, middle, middle, high, low)]
        else:
            rows += [high, middle, high, middle, low, high]
    if target:
        rows += list(split(norm)) + [ones] * 3
    else:
        rows += [ones] * 3 + list(split(norm + soften))
    rows += [zeros] * (FEATURES - len(rows))
    for k, row in enumerate(rows):
        ref[:, k, :] = row


def kernel(
    multipoles,
    operators_hbm,
    parents,
    shifts_hbm,
    slots,
    lists,
    positions,
    charges,
    counts,
    near,
    local_out,
    potential_out,
    ops,
    shifts,
    halo_out,
    halo_in,
    back_out,
    back_in,
    chosen,
    relay,
    onward,
    table,
    features,
    sources,
    above,
    targets,
    charge_columns,
    present,
    sums,
    own_sums,
    above_sums,
    gathered,
    parent_columns,
    load_sem,
    halo_sem,
    back_sem,
    first_send,
    first_recv,
    second_send,
    second_recv,
):
    zone = lax.axis_index("zone")
    level = lax.axis_index("level")
    levels = lax.axis_size("level")
    place = zone % GROUP
    group = zone // GROUP

    def first_peer(d):
        return (group * GROUP + (place + d) % GROUP, level)

    def second_peer(d):
        return (((group + d) % GROUP) * GROUP + place, level)

    up = (zone, (level + 1) % levels)
    down = (zone, (level + levels - 1) % levels)

    barrier = pltpu.get_barrier_semaphore()
    for peer in [down, up] + [first_peer(d) for d in range(1, GROUP)] + [
        second_peer(d) for d in range(1, GROUP)
    ]:
        pl.semaphore_signal(barrier, inc=1, device_id=peer, device_id_type=MESH)

    load_ops = pltpu.make_async_copy(operators_hbm, ops, load_sem.at[0])
    load_ops.start()
    load_shifts = pltpu.make_async_copy(shifts_hbm, shifts, load_sem.at[1])
    load_shifts.start()

    diagonal = iota((BOX, BOX), 0) == iota((BOX, BOX), 1)
    count_row = counts[...].reshape(1, BOX).astype(F32)
    count_column = jnp.sum(jnp.where(diagonal, count_row, 0.0), axis=1, keepdims=True)
    occupied = iota((BOX, S), 1).astype(F32) < count_column
    for c in range(3):
        x = positions[c]
        halo_out[c] = jnp.where(occupied, x, x[:, 0:1])
    halo_out[3] = jnp.where(occupied, charges[...], 0.0)

    own = jnp.concatenate(
        [multipoles[...], jnp.zeros((BOX, HALF - P2), BF16)], axis=1
    )
    r = iota((S, 64), 0)
    reader = (r // 4) % GROUP * GROUP + r // ROWS
    slot_rows = dot_t(flag(reader == iota((S, 64), 1)), slots[0].astype(F32).astype(BF16))
    mine = iota((S, 4), 0) % 4 == iota((S, 4), 1)
    picked = jnp.where(mine, slot_rows, 0.0).astype(BF16)
    box_of = dot(picked, jnp.ones((4, BOX), BF16))
    one_hot = flag(box_of == iota((S, BOX), 1).astype(F32))
    chosen[...] = dot(one_hot, own).astype(BF16).reshape(GROUP, ROWS, HALF)

    pl.semaphore_wait(barrier, 2 * GROUP)

    halo_copy = pltpu.make_async_remote_copy(
        src_ref=halo_out,
        dst_ref=halo_in,
        send_sem=halo_sem.at[0],
        recv_sem=halo_sem.at[1],
        device_id=down,
        device_id_type=MESH,
    )
    back_copy = pltpu.make_async_remote_copy(
        src_ref=back_out,
        dst_ref=back_in,
        send_sem=back_sem.at[0],
        recv_sem=back_sem.at[1],
        device_id=up,
        device_id_type=MESH,
    )

    @pl.when(level > 0)
    def _():
        halo_copy.start()

    def first_copy(d, slot):
        return pltpu.make_async_remote_copy(
            src_ref=chosen.at[(place + d) % GROUP],
            dst_ref=relay.at[slot],
            send_sem=first_send.at[d - 1],
            recv_sem=first_recv.at[d - 1],
            device_id=first_peer(d),
            device_id_type=MESH,
        )

    def second_copy(d, slot):
        return pltpu.make_async_remote_copy(
            src_ref=onward.at[(group + d) % GROUP],
            dst_ref=table.at[slot],
            send_sem=second_send.at[d - 1],
            recv_sem=second_recv.at[d - 1],
            device_id=second_peer(d),
            device_id_type=MESH,
        )

    for d in range(1, GROUP):
        first_copy(d, place).start()
    relay[place] = chosen[place]

    middle = [jnp.sum(halo_out[c, :, 0:1], axis=0, keepdims=True) * (1.0 / BOX) for c in range(3)]
    offsets = [halo_out[c] - middle[c] for c in range(3)]
    identity = flag(iota((S, S), 0) == iota((S, S), 1))
    write_features(features, offsets, True)

    def prepare(b, carry):
        targets[b] = dot_t(identity, features[b].astype(BF16)).astype(BF16)
        row = jnp.broadcast_to(halo_out[3, pl.ds(b, 1), :], (HALF, S))
        charge_columns[b] = row.T
        sums[b] = jnp.zeros((S, HALF), F32)
        return carry

    lax.fori_loop(0, BOX, prepare, 0)
    write_features(features, offsets, False)
    sources[...] = features[...].astype(BF16)
    own_sums[...] = jnp.zeros_like(own_sums)
    above_sums[...] = jnp.zeros_like(above_sums)
    hits = flag(near[...][:, None, :] == iota((BOX, WINDOW, NEAR), 1))
    present[...] = dot(
        hits.reshape(BOX * WINDOW, NEAR), jnp.ones((NEAR, HALF), BF16)
    ).reshape(BOX, WINDOW, HALF)

    def block(b, n, shift, side, charge, other):
        y = lax.rsqrt(dot(targets[b], side[n]))
        if other is None:
            y = jnp.where(iota((S, S), 0) == iota((S, S), 1), 0.0, y)
        there = present[b, pl.ds(shift + n, 1), :]
        row = charge[3, pl.ds(n, 1), :]
        left, right = y[:, :HALF], y[:, HALF:]
        sums[b] = sums[b] + (left * (row[:, :HALF] * there) + right * (row[:, HALF:] * there))
        if other is not None:
            column = charge_columns[b]
            for half, part in ((0, left), (HALF, right)):
                total = (part * column).reshape(S // 8, 8, HALF).sum(0)
                other[n, :, half : half + HALF] = (
                    other[n, :, half : half + HALF] + total * there
                )

    def own_block(b, n):
        block(b, n, BOX, sources, halo_out, own_sums)

    def own_pairs(s, carry):
        for w in range(4):
            own_block(code(s, w), code(s + 1, w))
            own_block(code(w, s), code(w, s + 1))
        for w in range(3):
            own_block(code(s, w), code(s + 1, w + 1))
            own_block(code(s + 1, w), code(s, w + 1))
        return carry

    def self_pairs(s, carry):
        for w in range(4):
            block(4 * s + w, 4 * s + w, BOX, sources, halo_out, None)
        return carry

    lax.fori_loop(0, 3, own_pairs, 0)

    for d in range(1, GROUP):
        first_copy(d, (place + GROUP - d) % GROUP).wait_recv()
    r0 = iota((S, S), 0)
    wanted = (r0 // 4) % GROUP * ROWS + r0 // ROWS * 4 + r0 % 4
    order = flag(wanted == iota((S, S), 1))
    onward[...] = (
        dot(order, relay[...].reshape(S, HALF)).astype(BF16).reshape(GROUP, ROWS, HALF)
    )
    for d in range(1, GROUP):
        second_copy(d, group).start()
    table[group] = onward[group]

    @pl.when(level < levels - 1)
    def _():
        halo_copy.wait_recv()
        write_features(features, [halo_in[c] - middle[c] for c in range(3)], False)
        above[...] = features[...].astype(BF16)

        def above_pairs(t, carry):
            x = (t + 1) // 3
            x_next = t - 2 * x
            for w in range(10):
                y = (w + 1) // 3
                y_next = w - 2 * y
                block(code(x, y), code(x_next, y_next), 2 * BOX, above, halo_in, above_sums)
            return carry

        lax.fori_loop(0, 10, above_pairs, 0)
        back_out[...] = jnp.sum(above_sums[...], axis=1)
        back_copy.start()

    lax.fori_loop(0, 4, self_pairs, 0)

    for d in range(1, GROUP):
        second_copy(d, (group + GROUP - d) % GROUP).wait_recv()
    whole = jnp.concatenate(
        [own, table[...].reshape(S, HALF), jnp.zeros((TABLE - S - BOX, HALF), BF16)], axis=0
    )
    columns = whole.T
    box_row = iota((TABLE, OFFSETS), 0)
    for b in range(BOX):
        named = flag(box_row == lists[b : b + 1, :])
        gathered[:, b, :] = dot(columns, named)

    load_ops.wait()

    def translate(s, total):
        for w in range(11):
            p = s * 11 + w
            total = total + dot(gathered[p].astype(BF16), ops[p])
        return total

    far = lax.fori_loop(0, P2 // 11, translate, jnp.zeros((BOX, P2), F32))

    load_shifts.wait()
    for g in range(2):
        row = jnp.concatenate([parents[g : g + 1, :], jnp.zeros((1, HALF - P2), F32)], axis=1)
        parent_columns[g] = jnp.broadcast_to(row, (HALF, HALF)).T
    downward = []
    for g in range(2):
        total = jnp.zeros((8, P2), F32)
        for p in range(P2):
            total = total + parent_columns[g, p : p + 1, :P2] * shifts[p]
        downward.append(total)
    local_out[...] = far + jnp.concatenate(downward, axis=0)

    def finish(b, carry):
        mine = jnp.sum(sums[b].T, axis=0, keepdims=True)
        theirs = jnp.sum(own_sums[b], axis=0, keepdims=True)
        potential_out[pl.ds(b, 1), :] = mine + theirs
        return carry

    lax.fori_loop(0, BOX, finish, 0)

    @pl.when(level > 0)
    def _():
        back_copy.wait_recv()
        potential_out[...] = potential_out[...] + back_in[...]
        halo_copy.wait_send()

    @pl.when(level < levels - 1)
    def _():
        back_copy.wait_send()

    potential_out[...] = jnp.where(occupied, potential_out[...], 0.0)
    for d in range(1, GROUP):
        first_copy(d, place).wait_send()
        second_copy(d, group).wait_send()


def per_device(
    multipoles,
    operators,
    parent_locals,
    shifts,
    send_slots,
    lists,
    positions,
    charges,
    counts,
    near_lists,
):
    arguments = (
        multipoles,
        operators.transpose(1, 0, 2),
        parent_locals,
        shifts.transpose(1, 0, 2),
        send_slots.transpose(0, 2, 1),
        lists,
        positions.transpose(1, 0, 2),
        charges,
        counts,
        near_lists,
    )
    vmem = pl.BlockSpec(memory_space=pltpu.VMEM)
    anywhere = pl.BlockSpec(memory_space=pl.ANY)
    specs = [vmem, anywhere, vmem, anywhere, vmem, vmem, vmem, vmem, vmem, vmem]
    return pl.pallas_call(
        kernel,
        out_shape=(
            jax.ShapeDtypeStruct((BOX, P2), F32),
            jax.ShapeDtypeStruct((BOX, S), F32),
        ),
        in_specs=specs,
        out_specs=(vmem, vmem),
        scratch_shapes=[
            pltpu.VMEM((P2, OFFSETS, P2), BF16),
            pltpu.VMEM((P2, 8, P2), F32),
            pltpu.VMEM((4, BOX, S), F32),
            pltpu.VMEM((4, BOX, S), F32),
            pltpu.VMEM((BOX, S), F32),
            pltpu.VMEM((BOX, S), F32),
            pltpu.VMEM((GROUP, ROWS, HALF), BF16),
            pltpu.VMEM((GROUP, ROWS, HALF), BF16),
            pltpu.VMEM((GROUP, ROWS, HALF), BF16),
            pltpu.VMEM((GROUP, ROWS, HALF), BF16),
            pltpu.VMEM((BOX, FEATURES, S), F32),
            pltpu.VMEM((BOX, FEATURES, S), BF16),
            pltpu.VMEM((BOX, FEATURES, S), BF16),
            pltpu.VMEM((BOX, S, FEATURES), BF16),
            pltpu.VMEM((BOX, S, HALF), F32),
            pltpu.VMEM((BOX, WINDOW, HALF), F32),
            pltpu.VMEM((BOX, S, HALF), F32),
            pltpu.VMEM((BOX, 8, S), F32),
            pltpu.VMEM((BOX, 8, S), F32),
            pltpu.VMEM((HALF, BOX, OFFSETS), F32),
            pltpu.VMEM((2, HALF, HALF), F32),
            pltpu.SemaphoreType.DMA((2,)),
            pltpu.SemaphoreType.DMA((2,)),
            pltpu.SemaphoreType.DMA((2,)),
            pltpu.SemaphoreType.DMA((GROUP - 1,)),
            pltpu.SemaphoreType.DMA((GROUP - 1,)),
            pltpu.SemaphoreType.DMA((GROUP - 1,)),
            pltpu.SemaphoreType.DMA((GROUP - 1,)),
        ],
        compiler_params=pltpu.CompilerParams(
            collective_id=0, has_side_effects=True, vmem_limit_bytes=48 * 2**20
        ),
    )(*arguments)


def solution(mesh):
    placed = (
        P(("zone", "level"), None),
        P(),
        P(("zone", "level"), None),
        P(),
        P(("zone", "level"), None, None),
        P(("zone", "level"), None),
        P(("zone", "level"), None, None),
        P(("zone", "level"), None),
        P(("zone", "level")),
        P(("zone", "level"), None),
    )
    return jax.shard_map(
        per_device,
        mesh=mesh,
        in_specs=placed,
        out_specs=(P(("zone", "level"), None), P(("zone", "level"), None)),
        check_vma=False,
    )
```

```python
import jax
import jax.numpy as jnp
from jax import lax
from jax.experimental import pallas as pl
from jax.experimental.pallas import tpu as pltpu
from jax.sharding import PartitionSpec as P

soften = 0.0025
BOX = 16
S = 256
HALF = 128
FEATURES = 32
NEAR = 27
WINDOW = 48
OFFSETS = 189
P2 = 121
DEPTH = 32
EXCEPTION = 45
MESH = pl.DeviceIdType.MESH
F32 = jnp.float32
BF16 = jnp.bfloat16


def iota(shape, dim):
    return lax.broadcasted_iota(jnp.int32, shape, dim)


def flag(mask, kind=BF16):
    return jnp.where(mask, 1.0, 0.0).astype(kind)


def dot(a, b):
    return jnp.dot(a, b, preferred_element_type=F32)


def dot_t(a, b):
    return lax.dot_general(a, b, (((1,), (1,)), ((), ())), preferred_element_type=F32)


def code(across, along):
    return across % 2 + 4 * (across // 2) + 2 * (along % 2) + 8 * (along // 2)


def split(x):
    high = x.astype(BF16).astype(F32)
    rest = x - high
    middle = rest.astype(BF16).astype(F32)
    return high, middle, rest - middle


def write_features(ref, coordinates, target):
    parts = [split(u) for u in coordinates]
    norm = coordinates[0] * coordinates[0]
    for u in coordinates[1:]:
        norm = norm + u * u
    ones = jnp.ones_like(norm)
    zeros = jnp.zeros_like(norm)
    rows = []
    for high, middle, low in parts:
        if target:
            rows += [-2.0 * r for r in (high, high, middle, middle, high, low)]
        else:
            rows += [high, middle, high, middle, low, high]
    if target:
        rows += list(split(norm)) + [ones] * 3
    else:
        rows += [ones] * 3 + list(split(norm + soften))
    rows += [zeros] * (FEATURES - len(rows))
    for k, row in enumerate(rows):
        ref[:, k, :] = row


def step(a, b):
    return (a + 64 - b) // 64


def first_level(level, levels):
    return (levels - 1 - level) // (levels - 1)


def zone_at(rank, level, levels):
    first = first_level(level, levels)
    at, after = step(rank, EXCEPTION), step(rank, EXCEPTION + 1)
    base = (rank + first * (1 - at)) * (1 - first * (at - after))
    distance = (base + 2) // 4
    side = ((base + 2) % 4) // 2
    z = (distance + side * (DEPTH - 2 * distance)) % DEPTH
    return 2 * z + base % 2


def rank_of(zone, level, levels):
    first = first_level(level, levels)
    z = zone // 2
    side = step(z, DEPTH // 2 + 1)
    distance = z + side * (DEPTH - 2 * z)
    base = 4 * distance - 2 + 2 * side + zone % 2 + 2 * (1 - step(z, 1))
    inside = step(base, 1)
    return base - first * (inside - step(base, EXCEPTION + 1)) + first * EXCEPTION * (1 - inside)


def kernel(
    multipoles_hbm,
    operators_hbm,
    parents_hbm,
    shifts_hbm,
    slots_hbm,
    lists_hbm,
    positions_hbm,
    charges_hbm,
    counts_hbm,
    near_hbm,
    local_out,
    potential_out,
    multipoles,
    ops,
    parents,
    shifts,
    slots,
    lists,
    positions,
    charges,
    counts,
    near,
    halo_out,
    halo_in,
    back_out,
    back_in,
    chosen,
    table,
    features,
    sources,
    below,
    targets,
    charge_columns,
    present,
    sums,
    own_sums,
    below_sums,
    named,
    gathered,
    parent_columns,
    load_sem,
    halo_sem,
    back_sem,
    slot_send,
    slot_recv,
):
    zone = lax.axis_index("zone")
    level = lax.axis_index("level")
    levels = lax.axis_size("level")
    zones = lax.axis_size("zone")
    rank = rank_of(zone, level, levels)

    loads = {}
    for k, (name, source, place) in enumerate(
        (
            ("multipoles", multipoles_hbm, multipoles),
            ("slots", slots_hbm, slots),
            ("counts", counts_hbm, counts),
            ("positions", positions_hbm, positions),
            ("charges", charges_hbm, charges),
            ("near", near_hbm, near),
            ("lists", lists_hbm, lists),
            ("parents", parents_hbm, parents),
            ("shifts", shifts_hbm, shifts),
            ("ops", operators_hbm, ops),
        )
    ):
        loads[name] = pltpu.make_async_copy(source, place, load_sem.at[k])
        loads[name].start()

    barrier = pltpu.get_barrier_semaphore()

    def tell(r, carry):
        pl.semaphore_signal(
            barrier, inc=1, device_id=(zone_at(r, level, levels), level), device_id_type=MESH
        )
        return carry

    lax.fori_loop(rank + 1, zones, tell, 0)

    @pl.when(level > 0)
    def _():
        pl.semaphore_signal(barrier, inc=1, device_id=(zone, level - 1), device_id_type=MESH)

    loads["multipoles"].wait()
    loads["slots"].wait()
    own = jnp.concatenate(
        [multipoles[...], jnp.zeros((BOX, HALF - P2), BF16)], axis=1
    )
    reader = iota((S, 64), 0) // 4
    slot_rows = dot_t(flag(reader == iota((S, 64), 1)), slots[0].astype(F32).astype(BF16))
    mine = iota((S, 4), 0) % 4 == iota((S, 4), 1)
    picked = jnp.where(mine, slot_rows, 0.0).astype(BF16)
    box_of = dot(picked, jnp.ones((4, BOX), BF16))
    one_hot = flag(box_of == iota((S, BOX), 1).astype(F32))
    chosen[...] = dot(one_hot, own).reshape(64, 4, HALF).astype(BF16)

    def slot_copy(source, place, peer):
        return pltpu.make_async_remote_copy(
            src_ref=chosen.at[source],
            dst_ref=table.at[place],
            send_sem=slot_send,
            recv_sem=slot_recv.at[place],
            device_id=(peer, level),
            device_id_type=MESH,
        )

    def send(r, carry):
        peer = zone_at(r, level, levels)
        slot_copy(peer, zone, peer).start()
        return carry

    def collect(r, carry):
        peer = zone_at(r, level, levels)
        slot_copy(peer, peer, peer).wait_recv()
        return carry

    def answer(r, carry):
        collect(r, carry)
        return send(r, carry)

    top = level // (levels - 1)

    @pl.when(rank + 1 - top > 0)
    def _():
        pl.semaphore_wait(barrier, rank + 1 - top)

    lax.fori_loop(0, rank, send, 0)
    table[zone] = chosen[zone]

    for name in ("counts", "positions", "charges"):
        loads[name].wait()
    diagonal = iota((BOX, BOX), 0) == iota((BOX, BOX), 1)
    count_row = counts[...].reshape(1, BOX).astype(F32)
    count_column = jnp.sum(jnp.where(diagonal, count_row, 0.0), axis=1, keepdims=True)
    occupied = iota((BOX, S), 1).astype(F32) < count_column
    for c in range(3):
        x = positions[c]
        halo_out[c] = jnp.where(occupied, x, x[:, 0:1])
    halo_out[3] = jnp.where(occupied, charges[...], 0.0)

    halo_copy = pltpu.make_async_remote_copy(
        src_ref=halo_out,
        dst_ref=halo_in,
        send_sem=halo_sem.at[0],
        recv_sem=halo_sem.at[1],
        device_id=(zone, (level + 1) % levels),
        device_id_type=MESH,
    )
    back_copy = pltpu.make_async_remote_copy(
        src_ref=back_out,
        dst_ref=back_in,
        send_sem=back_sem.at[0],
        recv_sem=back_sem.at[1],
        device_id=(zone, (level + levels - 1) % levels),
        device_id_type=MESH,
    )

    @pl.when(level < levels - 1)
    def _():
        halo_copy.start()

    middle = [jnp.sum(halo_out[c, :, 0:1], axis=0, keepdims=True) * (1.0 / BOX) for c in range(3)]
    offsets = [halo_out[c] - middle[c] for c in range(3)]
    identity = flag(iota((S, S), 0) == iota((S, S), 1))
    write_features(features, offsets, True)

    def prepare(b, carry):
        targets[b] = dot_t(identity, features[b].astype(BF16)).astype(BF16)
        row = jnp.broadcast_to(halo_out[3, pl.ds(b, 1), :], (HALF, S))
        charge_columns[b] = row.T
        sums[b] = jnp.zeros((S, HALF), F32)
        return carry

    lax.fori_loop(0, BOX, prepare, 0)
    write_features(features, offsets, False)
    sources[...] = features[...].astype(BF16)
    own_sums[...] = jnp.zeros_like(own_sums)
    below_sums[...] = jnp.zeros_like(below_sums)
    loads["near"].wait()
    hits = flag(near[...][:, None, :] == iota((BOX, WINDOW, NEAR), 1))
    present[...] = dot(
        hits.reshape(BOX * WINDOW, NEAR), jnp.ones((NEAR, HALF), BF16)
    ).reshape(BOX, WINDOW, HALF)

    def block(b, n, shift, side, charge, other):
        y = lax.rsqrt(dot(targets[b], side[n]))
        if other is None:
            y = jnp.where(iota((S, S), 0) == iota((S, S), 1), 0.0, y)
        there = present[b, pl.ds(shift + n, 1), :]
        row = charge[3, pl.ds(n, 1), :]
        left, right = y[:, :HALF], y[:, HALF:]
        sums[b] = sums[b] + (left * (row[:, :HALF] * there) + right * (row[:, HALF:] * there))
        if other is not None:
            column = charge_columns[b]
            for half, part in ((0, left), (HALF, right)):
                total = (part * column).reshape(S // 8, 8, HALF).sum(0)
                other[n, :, half : half + HALF] = (
                    other[n, :, half : half + HALF] + total * there
                )

    def own_block(b, n):
        block(b, n, BOX, sources, halo_out, own_sums)

    def own_pairs(s, carry):
        for w in range(4):
            own_block(code(s, w), code(s + 1, w))
            own_block(code(w, s), code(w, s + 1))
        for w in range(3):
            own_block(code(s, w), code(s + 1, w + 1))
            own_block(code(s + 1, w), code(s, w + 1))
        return carry

    def self_pairs(s, carry):
        for w in range(4):
            block(4 * s + w, 4 * s + w, BOX, sources, halo_out, None)
        return carry

    def below_pairs(t, carry):
        x = (t + 1) // 3
        x_next = t - 2 * x
        for w in range(10):
            y = (w + 1) // 3
            y_next = w - 2 * y
            block(code(x, y), code(x_next, y_next), 0, below, halo_in, below_sums)
        return carry

    lax.fori_loop(0, 3, own_pairs, 0)

    @pl.when(level > 0)
    def _():
        halo_copy.wait_recv()
        write_features(features, [halo_in[c] - middle[c] for c in range(3)], False)
        below[...] = features[...].astype(BF16)
        lax.fori_loop(0, 10, below_pairs, 0)
        back_out[...] = jnp.sum(below_sums[...], axis=1)
        back_copy.start()

    lax.fori_loop(0, 4, self_pairs, 0)

    loads["lists"].wait()
    own_columns = own.T
    for b in range(BOX):
        row = lists[b : b + 1, :]
        named[b] = flag(iota((S, OFFSETS), 0) + BOX == row)
        gathered[:, b, :] = dot(own_columns, flag(iota((BOX, OFFSETS), 0) == row))

    loads["parents"].wait()
    loads["shifts"].wait()
    for g in range(2):
        row = jnp.concatenate([parents[g : g + 1, :], jnp.zeros((1, HALF - P2), F32)], axis=1)
        parent_columns[g] = jnp.broadcast_to(row, (HALF, HALF)).T
    for g in range(2):
        total = jnp.zeros((8, P2), F32)
        for p in range(P2):
            total = total + parent_columns[g, p : p + 1, :P2] * shifts[p]
        local_out[8 * g : 8 * g + 8, :] = total

    def finish(b, carry):
        mine = jnp.sum(sums[b].T, axis=0, keepdims=True)
        theirs = jnp.sum(own_sums[b], axis=0, keepdims=True)
        potential_out[pl.ds(b, 1), :] = mine + theirs
        return carry

    lax.fori_loop(0, BOX, finish, 0)

    @pl.when(level < levels - 1)
    def _():
        back_copy.wait_recv()
        potential_out[...] = potential_out[...] + back_in[...]
        halo_copy.wait_send()

    @pl.when(level > 0)
    def _():
        back_copy.wait_send()

    potential_out[...] = jnp.where(occupied, potential_out[...], 0.0)
    loads["ops"].wait()

    lax.fori_loop(0, rank, collect, 0)
    lax.fori_loop(rank + 1, zones, answer, 0)
    columns = table[...].reshape(S, HALF).T
    for b in range(BOX):
        gathered[:, b, :] = gathered[:, b, :] + dot(columns, named[b])

    def translate(s, total):
        for w in range(11):
            p = s * 11 + w
            total = total + dot(gathered[p].astype(BF16), ops[p])
        return total

    far = lax.fori_loop(0, P2 // 11, translate, jnp.zeros((BOX, P2), F32), unroll=True)
    local_out[...] = local_out[...] + far
    pltpu.make_async_copy(chosen.at[pl.ds(1, 63)], chosen.at[pl.ds(1, 63)], slot_send).wait()


def per_device(
    multipoles,
    operators,
    parent_locals,
    shifts,
    send_slots,
    lists,
    positions,
    charges,
    counts,
    near_lists,
):
    arguments = (
        multipoles,
        operators.transpose(1, 0, 2),
        parent_locals,
        shifts.transpose(1, 0, 2),
        send_slots.transpose(0, 2, 1),
        lists,
        positions.transpose(1, 0, 2),
        charges,
        counts,
        near_lists,
    )
    vmem = pl.BlockSpec(memory_space=pltpu.VMEM)
    specs = [pl.BlockSpec(memory_space=pltpu.HBM)] * 10
    return pl.pallas_call(
        kernel,
        out_shape=(
            jax.ShapeDtypeStruct((BOX, P2), F32),
            jax.ShapeDtypeStruct((BOX, S), F32),
        ),
        in_specs=specs,
        out_specs=(vmem, vmem),
        scratch_shapes=[pltpu.VMEM(x.shape, x.dtype) for x in arguments]
        + [
            pltpu.VMEM((4, BOX, S), F32),
            pltpu.VMEM((4, BOX, S), F32),
            pltpu.VMEM((BOX, S), F32),
            pltpu.VMEM((BOX, S), F32),
            pltpu.VMEM((64, 4, HALF), BF16),
            pltpu.VMEM((64, 4, HALF), BF16),
            pltpu.VMEM((BOX, FEATURES, S), F32),
            pltpu.VMEM((BOX, FEATURES, S), BF16),
            pltpu.VMEM((BOX, FEATURES, S), BF16),
            pltpu.VMEM((BOX, S, FEATURES), BF16),
            pltpu.VMEM((BOX, S, HALF), F32),
            pltpu.VMEM((BOX, WINDOW, HALF), F32),
            pltpu.VMEM((BOX, S, HALF), F32),
            pltpu.VMEM((BOX, 8, S), F32),
            pltpu.VMEM((BOX, 8, S), F32),
            pltpu.VMEM((BOX, S, OFFSETS), BF16),
            pltpu.VMEM((HALF, BOX, OFFSETS), F32),
            pltpu.VMEM((2, HALF, HALF), F32),
            pltpu.SemaphoreType.DMA((10,)),
            pltpu.SemaphoreType.DMA((2,)),
            pltpu.SemaphoreType.DMA((2,)),
            pltpu.SemaphoreType.DMA,
            pltpu.SemaphoreType.DMA((64,)),
        ],
        compiler_params=pltpu.CompilerParams(
            collective_id=0, has_side_effects=True, vmem_limit_bytes=60 * 2**20
        ),
    )(*arguments)


def solution(mesh):
    placed = (
        P(("zone", "level"), None),
        P(),
        P(("zone", "level"), None),
        P(),
        P(("zone", "level"), None, None),
        P(("zone", "level"), None),
        P(("zone", "level"), None, None),
        P(("zone", "level"), None),
        P(("zone", "level")),
        P(("zone", "level"), None),
    )
    return jax.shard_map(
        per_device,
        mesh=mesh,
        in_specs=placed,
        out_specs=(P(("zone", "level"), None), P(("zone", "level"), None)),
        check_vma=False,
    )
```

```python
import jax
import jax.numpy as jnp
from jax import lax
from jax.experimental import pallas as pl
from jax.experimental.pallas import tpu as pltpu
from jax.sharding import PartitionSpec as P

soften = 0.0025
BOX = 16
S = 256
HALF = 128
FEATURES = 32
NEAR = 27
WINDOW = 48
OFFSETS = 189
P2 = 121
DEPTH = 32
EXCEPTION = 26
MESH = pl.DeviceIdType.MESH
F32 = jnp.float32
BF16 = jnp.bfloat16


def iota(shape, dim):
    return lax.broadcasted_iota(jnp.int32, shape, dim)


def flag(mask, kind=BF16):
    return jnp.where(mask, 1.0, 0.0).astype(kind)


def dot(a, b):
    return jnp.dot(a, b, preferred_element_type=F32)


def dot_t(a, b):
    return lax.dot_general(a, b, (((1,), (1,)), ((), ())), preferred_element_type=F32)


def code(across, along):
    return across % 2 + 4 * (across // 2) + 2 * (along % 2) + 8 * (along // 2)


def split(x):
    high = x.astype(BF16).astype(F32)
    rest = x - high
    middle = rest.astype(BF16).astype(F32)
    return high, middle, rest - middle


def write_features(ref, coordinates, target):
    parts = [split(u) for u in coordinates]
    norm = coordinates[0] * coordinates[0]
    for u in coordinates[1:]:
        norm = norm + u * u
    ones = jnp.ones_like(norm)
    zeros = jnp.zeros_like(norm)
    rows = []
    for high, middle, low in parts:
        if target:
            rows += [-2.0 * r for r in (high, high, middle, middle, high, low)]
        else:
            rows += [high, middle, high, middle, low, high]
    if target:
        rows += list(split(norm)) + [ones] * 3
    else:
        rows += [ones] * 3 + list(split(norm + soften))
    rows += [zeros] * (FEATURES - len(rows))
    for k, row in enumerate(rows):
        ref[:, k, :] = row


def step(a, b):
    return (a + 64 - b) // 64


def first_level(level, levels):
    return (levels - 1 - level) // (levels - 1)


def zone_at(rank, level, levels):
    first = first_level(level, levels)
    at, after = step(rank, EXCEPTION), step(rank, EXCEPTION + 1)
    base = (rank + first * (1 - at)) * (1 - first * (at - after))
    upper = step(base, DEPTH)
    z = base // 2 + upper * (3 * DEPTH // 2 - 1 - 2 * (base // 2))
    return 2 * z + base % 2


def rank_of(zone, level, levels):
    first = first_level(level, levels)
    z = zone // 2
    base = 2 * (z + step(z, DEPTH // 2) * (3 * DEPTH // 2 - 1 - 2 * z)) + zone % 2
    inside = step(base, 1)
    return base - first * (inside - step(base, EXCEPTION + 1)) + first * EXCEPTION * (1 - inside)


def kernel(
    multipoles_hbm,
    operators_hbm,
    parents_hbm,
    shifts_hbm,
    slots_hbm,
    lists_hbm,
    positions_hbm,
    charges_hbm,
    counts_hbm,
    near_hbm,
    local_out,
    potential_out,
    multipoles,
    ops,
    parents,
    shifts,
    slots,
    lists,
    positions,
    charges,
    counts,
    near,
    halo_out,
    halo_in,
    back_out,
    back_in,
    chosen,
    table,
    features,
    sources,
    below,
    targets,
    charge_columns,
    present,
    sums,
    own_sums,
    below_sums,
    named,
    gathered,
    parent_columns,
    load_sem,
    halo_sem,
    back_sem,
    slot_send,
    slot_recv,
    ready,
):
    zone = lax.axis_index("zone")
    level = lax.axis_index("level")
    levels = lax.axis_size("level")
    zones = lax.axis_size("zone")
    rank = rank_of(zone, level, levels)

    loads = {}
    for k, (name, source, place) in enumerate(
        (
            ("multipoles", multipoles_hbm, multipoles),
            ("slots", slots_hbm, slots),
            ("counts", counts_hbm, counts),
            ("positions", positions_hbm, positions),
            ("charges", charges_hbm, charges),
            ("near", near_hbm, near),
            ("lists", lists_hbm, lists),
            ("parents", parents_hbm, parents),
            ("shifts", shifts_hbm, shifts),
            ("ops", operators_hbm, ops),
        )
    ):
        loads[name] = pltpu.make_async_copy(source, place, load_sem.at[k])
        loads[name].start()

    barrier = pltpu.get_barrier_semaphore()

    def tell(r, carry):
        pl.semaphore_signal(
            barrier, inc=1, device_id=(zone_at(r, level, levels), level), device_id_type=MESH
        )
        return carry

    lax.fori_loop(rank + 1, zones, tell, 0)

    @pl.when(level > 0)
    def _():
        pl.semaphore_signal(barrier, inc=1, device_id=(zone, level - 1), device_id_type=MESH)

    top = level // (levels - 1)

    @pl.when(rank + 1 - top > 0)
    def _():
        pl.semaphore_wait(barrier, rank + 1 - top)

    def greet(r, carry):
        pl.semaphore_signal(
            ready, inc=1, device_id=(zone_at(r, level, levels), level), device_id_type=MESH
        )
        return carry

    lax.fori_loop(0, rank, greet, 0)

    loads["multipoles"].wait()
    loads["slots"].wait()
    own = jnp.concatenate(
        [multipoles[...], jnp.zeros((BOX, HALF - P2), BF16)], axis=1
    )
    reader = iota((S, 64), 0) // 4
    slot_rows = dot_t(flag(reader == iota((S, 64), 1)), slots[0].astype(F32).astype(BF16))
    mine = iota((S, 4), 0) % 4 == iota((S, 4), 1)
    picked = jnp.where(mine, slot_rows, 0.0).astype(BF16)
    box_of = dot(picked, jnp.ones((4, BOX), BF16))
    one_hot = flag(box_of == iota((S, BOX), 1).astype(F32))
    chosen[...] = dot(one_hot, own).reshape(64, 4, HALF).astype(BF16)

    def slot_copy(source, place, peer):
        return pltpu.make_async_remote_copy(
            src_ref=chosen.at[source],
            dst_ref=table.at[place],
            send_sem=slot_send,
            recv_sem=slot_recv.at[place],
            device_id=(peer, level),
            device_id_type=MESH,
        )

    def send(r, carry):
        peer = zone_at(r, level, levels)
        slot_copy(peer, zone, peer).start()
        return carry

    def collect(r, carry):
        peer = zone_at(r, level, levels)
        slot_copy(peer, peer, peer).wait_recv()
        return carry

    lax.fori_loop(0, rank, send, 0)
    table[zone] = chosen[zone]

    for name in ("counts", "positions", "charges"):
        loads[name].wait()
    diagonal = iota((BOX, BOX), 0) == iota((BOX, BOX), 1)
    count_row = counts[...].reshape(1, BOX).astype(F32)
    count_column = jnp.sum(jnp.where(diagonal, count_row, 0.0), axis=1, keepdims=True)
    occupied = iota((BOX, S), 1).astype(F32) < count_column
    for c in range(3):
        x = positions[c]
        halo_out[c] = jnp.where(occupied, x, x[:, 0:1])
    halo_out[3] = jnp.where(occupied, charges[...], 0.0)

    halo_copy = pltpu.make_async_remote_copy(
        src_ref=halo_out,
        dst_ref=halo_in,
        send_sem=halo_sem.at[0],
        recv_sem=halo_sem.at[1],
        device_id=(zone, (level + 1) % levels),
        device_id_type=MESH,
    )
    back_copy = pltpu.make_async_remote_copy(
        src_ref=back_out,
        dst_ref=back_in,
        send_sem=back_sem.at[0],
        recv_sem=back_sem.at[1],
        device_id=(zone, (level + levels - 1) % levels),
        device_id_type=MESH,
    )

    @pl.when(level < levels - 1)
    def _():
        halo_copy.start()

    middle = [jnp.sum(halo_out[c, :, 0:1], axis=0, keepdims=True) * (1.0 / BOX) for c in range(3)]
    offsets = [halo_out[c] - middle[c] for c in range(3)]
    identity = flag(iota((S, S), 0) == iota((S, S), 1))
    write_features(features, offsets, True)

    def prepare(b, carry):
        targets[b] = dot_t(identity, features[b].astype(BF16)).astype(BF16)
        row = jnp.broadcast_to(halo_out[3, pl.ds(b, 1), :], (HALF, S))
        charge_columns[b] = row.T
        sums[b] = jnp.zeros((S, HALF), F32)
        return carry

    lax.fori_loop(0, BOX, prepare, 0)
    write_features(features, offsets, False)
    sources[...] = features[...].astype(BF16)
    own_sums[...] = jnp.zeros_like(own_sums)
    below_sums[...] = jnp.zeros_like(below_sums)
    loads["near"].wait()
    hits = flag(near[...][:, None, :] == iota((BOX, WINDOW, NEAR), 1))
    present[...] = dot(
        hits.reshape(BOX * WINDOW, NEAR), jnp.ones((NEAR, HALF), BF16)
    ).reshape(BOX, WINDOW, HALF)

    def block(b, n, shift, side, charge, other):
        y = lax.rsqrt(dot(targets[b], side[n]))
        if other is None:
            y = jnp.where(iota((S, S), 0) == iota((S, S), 1), 0.0, y)
        there = present[b, pl.ds(shift + n, 1), :]
        row = charge[3, pl.ds(n, 1), :]
        left, right = y[:, :HALF], y[:, HALF:]
        sums[b] = sums[b] + (left * (row[:, :HALF] * there) + right * (row[:, HALF:] * there))
        if other is not None:
            column = charge_columns[b]
            for half, part in ((0, left), (HALF, right)):
                total = (part * column).reshape(S // 8, 8, HALF).sum(0)
                other[n, :, half : half + HALF] = (
                    other[n, :, half : half + HALF] + total * there
                )

    def own_block(b, n):
        block(b, n, BOX, sources, halo_out, own_sums)

    def own_pairs(s, carry):
        for w in range(4):
            own_block(code(s, w), code(s + 1, w))
            own_block(code(w, s), code(w, s + 1))
        for w in range(3):
            own_block(code(s, w), code(s + 1, w + 1))
            own_block(code(s + 1, w), code(s, w + 1))
        return carry

    def self_pairs(s, carry):
        for w in range(4):
            block(4 * s + w, 4 * s + w, BOX, sources, halo_out, None)
        return carry

    def below_pairs(t, carry):
        x = (t + 1) // 3
        x_next = t - 2 * x
        for w in range(10):
            y = (w + 1) // 3
            y_next = w - 2 * y
            block(code(x, y), code(x_next, y_next), 0, below, halo_in, below_sums)
        return carry

    lax.fori_loop(0, 3, own_pairs, 0)

    @pl.when(level > 0)
    def _():
        halo_copy.wait_recv()
        write_features(features, [halo_in[c] - middle[c] for c in range(3)], False)
        below[...] = features[...].astype(BF16)
        lax.fori_loop(0, 10, below_pairs, 0)
        back_out[...] = jnp.sum(below_sums[...], axis=1)
        back_copy.start()

    lax.fori_loop(0, 4, self_pairs, 0)

    loads["lists"].wait()
    own_columns = own.T
    for b in range(BOX):
        row = lists[b : b + 1, :]
        named[b] = flag(iota((S, OFFSETS), 0) + BOX == row)
        gathered[:, b, :] = dot(own_columns, flag(iota((BOX, OFFSETS), 0) == row))

    loads["parents"].wait()
    loads["shifts"].wait()
    for g in range(2):
        row = jnp.concatenate([parents[g : g + 1, :], jnp.zeros((1, HALF - P2), F32)], axis=1)
        parent_columns[g] = jnp.broadcast_to(row, (HALF, HALF)).T
    for g in range(2):
        total = jnp.zeros((8, P2), F32)
        for p in range(P2):
            total = total + parent_columns[g, p : p + 1, :P2] * shifts[p]
        local_out[8 * g : 8 * g + 8, :] = total

    def finish(b, carry):
        mine = jnp.sum(sums[b].T, axis=0, keepdims=True)
        theirs = jnp.sum(own_sums[b], axis=0, keepdims=True)
        potential_out[pl.ds(b, 1), :] = mine + theirs
        return carry

    lax.fori_loop(0, BOX, finish, 0)

    @pl.when(level < levels - 1)
    def _():
        back_copy.wait_recv()
        potential_out[...] = potential_out[...] + back_in[...]
        halo_copy.wait_send()

    @pl.when(level > 0)
    def _():
        back_copy.wait_send()

    potential_out[...] = jnp.where(occupied, potential_out[...], 0.0)
    loads["ops"].wait()

    @pl.when(rank < zones - 1)
    def _():
        pl.semaphore_wait(ready, zones - 1 - rank)

    lax.fori_loop(rank + 1, zones, send, 0)
    lax.fori_loop(0, rank, collect, 0)
    lax.fori_loop(rank + 1, zones, collect, 0)
    columns = table[...].reshape(S, HALF).T
    for b in range(BOX):
        gathered[:, b, :] = gathered[:, b, :] + dot(columns, named[b])

    def translate(s, total):
        for w in range(11):
            p = s * 11 + w
            total = total + dot(gathered[p].astype(BF16), ops[p])
        return total

    far = lax.fori_loop(0, P2 // 11, translate, jnp.zeros((BOX, P2), F32), unroll=True)
    local_out[...] = local_out[...] + far
    pltpu.make_async_copy(chosen.at[pl.ds(1, 63)], chosen.at[pl.ds(1, 63)], slot_send).wait()


def per_device(
    multipoles,
    operators,
    parent_locals,
    shifts,
    send_slots,
    lists,
    positions,
    charges,
    counts,
    near_lists,
):
    arguments = (
        multipoles,
        operators.transpose(1, 0, 2),
        parent_locals,
        shifts.transpose(1, 0, 2),
        send_slots.transpose(0, 2, 1),
        lists,
        positions.transpose(1, 0, 2),
        charges,
        counts,
        near_lists,
    )
    vmem = pl.BlockSpec(memory_space=pltpu.VMEM)
    specs = [pl.BlockSpec(memory_space=pltpu.HBM)] * 10
    return pl.pallas_call(
        kernel,
        out_shape=(
            pltpu.VMEM((BOX, P2), F32),
            pltpu.VMEM((BOX, S), F32),
        ),
        in_specs=specs,
        out_specs=(vmem, vmem),
        scratch_shapes=[pltpu.VMEM(x.shape, x.dtype) for x in arguments]
        + [
            pltpu.VMEM((4, BOX, S), F32),
            pltpu.VMEM((4, BOX, S), F32),
            pltpu.VMEM((BOX, S), F32),
            pltpu.VMEM((BOX, S), F32),
            pltpu.VMEM((64, 4, HALF), BF16),
            pltpu.VMEM((64, 4, HALF), BF16),
            pltpu.VMEM((BOX, FEATURES, S), F32),
            pltpu.VMEM((BOX, FEATURES, S), BF16),
            pltpu.VMEM((BOX, FEATURES, S), BF16),
            pltpu.VMEM((BOX, S, FEATURES), BF16),
            pltpu.VMEM((BOX, S, HALF), F32),
            pltpu.VMEM((BOX, WINDOW, HALF), F32),
            pltpu.VMEM((BOX, S, HALF), F32),
            pltpu.VMEM((BOX, 8, S), F32),
            pltpu.VMEM((BOX, 8, S), F32),
            pltpu.VMEM((BOX, S, OFFSETS), BF16),
            pltpu.VMEM((HALF, BOX, OFFSETS), F32),
            pltpu.VMEM((2, HALF, HALF), F32),
            pltpu.SemaphoreType.DMA((10,)),
            pltpu.SemaphoreType.DMA((2,)),
            pltpu.SemaphoreType.DMA((2,)),
            pltpu.SemaphoreType.DMA,
            pltpu.SemaphoreType.DMA((64,)),
            pltpu.SemaphoreType.REGULAR,
        ],
        compiler_params=pltpu.CompilerParams(
            collective_id=0, has_side_effects=True, vmem_limit_bytes=60 * 2**20
        ),
    )(*arguments)


def solution(mesh):
    placed = (
        P(("zone", "level"), None),
        P(),
        P(("zone", "level"), None),
        P(),
        P(("zone", "level"), None, None),
        P(("zone", "level"), None),
        P(("zone", "level"), None, None),
        P(("zone", "level"), None),
        P(("zone", "level")),
        P(("zone", "level"), None),
    )
    return jax.shard_map(
        per_device,
        mesh=mesh,
        in_specs=placed,
        out_specs=(P(("zone", "level"), None), P(("zone", "level"), None)),
        check_vma=False,
    )
```

```python
import jax
import jax.numpy as jnp
from jax import lax
from jax.experimental import pallas as pl
from jax.experimental.pallas import tpu as pltpu
from jax.sharding import PartitionSpec as P

soften = 0.0025
BOX = 16
S = 256
HALF = 128
FEATURES = 32
NEAR = 27
WINDOW = 48
OFFSETS = 189
P2 = 121
GROUP = 8
ZONES = 64
MOVED = 16
WORK_FIRST = 48
MESH = pl.DeviceIdType.MESH
F32 = jnp.float32
BF16 = jnp.bfloat16


def iota(shape, dim):
    return lax.broadcasted_iota(jnp.int32, shape, dim)


def flag(mask, kind=BF16):
    return jnp.where(mask, 1.0, 0.0).astype(kind)


def dot(a, b):
    return jnp.dot(a, b, preferred_element_type=F32)


def dot_t(a, b):
    return lax.dot_general(a, b, (((1,), (1,)), ((), ())), preferred_element_type=F32)


def code(across, along):
    return across % 2 + 4 * (across // 2) + 2 * (along % 2) + 8 * (along // 2)


def split(x):
    high = x.astype(BF16).astype(F32)
    rest = x - high
    middle = rest.astype(BF16).astype(F32)
    return high, middle, rest - middle


def write_features(ref, coordinates, target):
    parts = [split(u) for u in coordinates]
    norm = coordinates[0] * coordinates[0]
    for u in coordinates[1:]:
        norm = norm + u * u
    ones = jnp.ones_like(norm)
    zeros = jnp.zeros_like(norm)
    rows = []
    for high, middle, low in parts:
        if target:
            rows += [-2.0 * r for r in (high, high, middle, middle, high, low)]
        else:
            rows += [high, middle, high, middle, low, high]
    if target:
        rows += list(split(norm)) + [ones] * 3
    else:
        rows += [ones] * 3 + list(split(norm + soften))
    rows += [zeros] * (FEATURES - len(rows))
    for k, row in enumerate(rows):
        ref[:, k, :] = row


def over(low, high, body):
    def one(peer, carry):
        body(peer)
        return carry

    lax.fori_loop(low, high, one, 0)


def kernel(
    multipoles_hbm,
    operators_hbm,
    parents_hbm,
    shifts_hbm,
    slots_hbm,
    lists_hbm,
    positions_hbm,
    charges_hbm,
    counts_hbm,
    near_hbm,
    local_out,
    potential_out,
    multipoles,
    ops,
    parents,
    shifts,
    slots,
    lists,
    positions,
    charges,
    counts,
    near,
    halo_out,
    halo_in,
    back_out,
    back_in,
    chosen,
    table,
    features,
    sources,
    below,
    targets,
    charge_columns,
    present,
    sums,
    own_sums,
    below_sums,
    named,
    gathered,
    parent_columns,
    load_sem,
    halo_sem,
    back_sem,
    slot_send,
    slot_recv,
    ready,
):
    zone = lax.axis_index("zone")
    level = lax.axis_index("level")
    levels = lax.axis_size("level")
    group = zone // GROUP
    top = level // (levels - 1)
    first = (levels - 1 - level) // (levels - 1)
    origin = (ZONES - 1 - zone) // (ZONES - 1)
    moved = first * origin
    extra = first * (1 - origin) * ((ZONES + MOVED - 1 - zone) // ZONES)
    before = (extra + moved, zone + MOVED * moved)
    after = (zone + 1 + (MOVED - 1) * moved, ZONES)

    loads = {}
    for k, (name, source, held) in enumerate(
        (
            ("multipoles", multipoles_hbm, multipoles),
            ("slots", slots_hbm, slots),
            ("counts", counts_hbm, counts),
            ("positions", positions_hbm, positions),
            ("charges", charges_hbm, charges),
            ("near", near_hbm, near),
            ("lists", lists_hbm, lists),
            ("parents", parents_hbm, parents),
            ("shifts", shifts_hbm, shifts),
            ("ops", operators_hbm, ops),
        )
    ):
        loads[name] = pltpu.make_async_copy(source, held, load_sem.at[k])
        loads[name].start()

    barrier = pltpu.get_barrier_semaphore()

    def signal(semaphore, zone_to, level_to):
        pl.semaphore_signal(
            semaphore, inc=1, device_id=(zone_to, level_to), device_id_type=MESH
        )

    @pl.when(level > 0)
    def _():
        signal(barrier, zone, level - 1)

    @pl.when(extra == 1)
    def _():
        signal(barrier, 0, level)

    over(*after, lambda peer: signal(barrier, peer, level))

    def slot_copy(source, place, peer):
        return pltpu.make_async_remote_copy(
            src_ref=chosen.at[source],
            dst_ref=table.at[place],
            send_sem=slot_send,
            recv_sem=slot_recv.at[place],
            device_id=(peer, level),
            device_id_type=MESH,
        )

    def send(peer):
        slot_copy(peer, zone, peer).start()

    def send_early(peer):
        send(peer)
        signal(ready.at[group + GROUP * moved], peer, level)

    def collect(peer):
        slot_copy(peer, peer, peer).wait_recv()

    loads["multipoles"].wait()
    loads["slots"].wait()
    own = jnp.concatenate([multipoles[...], jnp.zeros((BOX, HALF - P2), BF16)], axis=1)
    reader = iota((S, ZONES), 0) // 4
    slot_rows = dot_t(flag(reader == iota((S, ZONES), 1)), slots[0].astype(F32).astype(BF16))
    mine = iota((S, 4), 0) % 4 == iota((S, 4), 1)
    picked = jnp.where(mine, slot_rows, 0.0).astype(BF16)
    box_of = dot(picked, jnp.ones((4, BOX), BF16))
    one_hot = flag(box_of == iota((S, BOX), 1).astype(F32))
    chosen[...] = dot(one_hot, own).reshape(ZONES, 4, HALF).astype(BF16)

    for name in ("counts", "positions", "charges"):
        loads[name].wait()
    diagonal = iota((BOX, BOX), 0) == iota((BOX, BOX), 1)
    count_row = counts[...].reshape(1, BOX).astype(F32)
    count_column = jnp.sum(jnp.where(diagonal, count_row, 0.0), axis=1, keepdims=True)
    occupied = iota((BOX, S), 1).astype(F32) < count_column
    for c in range(3):
        x = positions[c]
        halo_out[c] = jnp.where(occupied, x, x[:, 0:1])
    halo_out[3] = jnp.where(occupied, charges[...], 0.0)

    halo_copy = pltpu.make_async_remote_copy(
        src_ref=halo_out,
        dst_ref=halo_in,
        send_sem=halo_sem.at[0],
        recv_sem=halo_sem.at[1],
        device_id=(zone, (level + 1) % levels),
        device_id_type=MESH,
    )
    back_copy = pltpu.make_async_remote_copy(
        src_ref=back_out,
        dst_ref=back_in,
        send_sem=back_sem.at[0],
        recv_sem=back_sem.at[1],
        device_id=(zone, (level + levels - 1) % levels),
        device_id_type=MESH,
    )

    middle = [jnp.sum(halo_out[c, :, 0:1], axis=0, keepdims=True) * (1.0 / BOX) for c in range(3)]

    def block(b, n, shift, side, charge, other):
        y = lax.rsqrt(dot(targets[b], side[n]))
        if other is None:
            y = jnp.where(iota((S, S), 0) == iota((S, S), 1), 0.0, y)
        there = present[b, pl.ds(shift + n, 1), :]
        row = charge[3, pl.ds(n, 1), :]
        left, right = y[:, :HALF], y[:, HALF:]
        sums[b] = sums[b] + (left * (row[:, :HALF] * there) + right * (row[:, HALF:] * there))
        if other is not None:
            column = charge_columns[b]
            for half, part in ((0, left), (HALF, right)):
                total = (part * column).reshape(S // 8, 8, HALF).sum(0)
                other[n, :, half : half + HALF] = (
                    other[n, :, half : half + HALF] + total * there
                )

    def own_block(b, n):
        block(b, n, BOX, sources, halo_out, own_sums)

    def own_pairs(s, carry):
        for w in range(4):
            own_block(code(s, w), code(s + 1, w))
            own_block(code(w, s), code(w, s + 1))
        for w in range(3):
            own_block(code(s, w), code(s + 1, w + 1))
            own_block(code(s + 1, w), code(s, w + 1))
        return carry

    def self_pairs(s, carry):
        for w in range(4):
            block(4 * s + w, 4 * s + w, BOX, sources, halo_out, None)
        return carry

    def below_pairs(t, carry):
        x = (t + 1) // 3
        x_next = t - 2 * x
        for w in range(10):
            y = (w + 1) // 3
            y_next = w - 2 * y
            block(code(x, y), code(x_next, y_next), 0, below, halo_in, below_sums)
        return carry

    def prepare_and_pair():
        offsets = [halo_out[c] - middle[c] for c in range(3)]
        identity = flag(iota((S, S), 0) == iota((S, S), 1))
        write_features(features, offsets, True)

        def prepare(b, carry):
            targets[b] = dot_t(identity, features[b].astype(BF16)).astype(BF16)
            row = jnp.broadcast_to(halo_out[3, pl.ds(b, 1), :], (HALF, S))
            charge_columns[b] = row.T
            sums[b] = jnp.zeros((S, HALF), F32)
            return carry

        lax.fori_loop(0, BOX, prepare, 0)
        write_features(features, offsets, False)
        sources[...] = features[...].astype(BF16)
        own_sums[...] = jnp.zeros_like(own_sums)
        below_sums[...] = jnp.zeros_like(below_sums)
        loads["near"].wait()
        hits = flag(near[...][:, None, :] == iota((BOX, WINDOW, NEAR), 1))
        present[...] = dot(
            hits.reshape(BOX * WINDOW, NEAR), jnp.ones((NEAR, HALF), BF16)
        ).reshape(BOX, WINDOW, HALF)

        lax.fori_loop(0, 3, own_pairs, 0)

    def name_members():
        loads["lists"].wait()
        own_columns = own.T
        entry = BOX + iota((S, OFFSETS), 0)
        for b in range(BOX):
            row = lists[b : b + 1, :]
            named[b] = flag(entry == row)
            gathered[:, b, :] = dot(own_columns, flag(iota((BOX, OFFSETS), 0) == row))

        loads["parents"].wait()
        loads["shifts"].wait()
        for g in range(2):
            row = jnp.concatenate([parents[g : g + 1, :], jnp.zeros((1, HALF - P2), F32)], axis=1)
            parent_columns[g] = jnp.broadcast_to(row, (HALF, HALF)).T
        for g in range(2):
            total = jnp.zeros((8, P2), F32)
            for p in range(P2):
                total = total + parent_columns[g, p : p + 1, :P2] * shifts[p]
            local_out[8 * g : 8 * g + 8, :] = total

    def send_first():
        count_before = before[1] - before[0]

        @pl.when(count_before + 1 - top > 0)
        def _():
            pl.semaphore_wait(barrier, count_before + 1 - top)

        over(*before, send_early)
        table[zone] = chosen[zone]

        @pl.when(level < levels - 1)
        def _():
            halo_copy.start()

    here = 1 - (zone + ZONES - WORK_FIRST) // ZONES

    def phase(k, carry):
        @pl.when(k == here)
        def _():
            prepare_and_pair()

        @pl.when(k == 1 - here)
        def _():
            send_first()

        return carry

    lax.fori_loop(0, 2, phase, 0)
    lax.fori_loop(0, 4, self_pairs, 0)
    name_members()

    @pl.when(level > 0)
    def _():
        halo_copy.wait_recv()
        write_features(features, [halo_in[c] - middle[c] for c in range(3)], False)
        below[...] = features[...].astype(BF16)
        lax.fori_loop(0, 10, below_pairs, 0)
        back_out[...] = jnp.sum(below_sums[...], axis=1)
        back_copy.start()

    def finish(b, carry):
        mine = jnp.sum(sums[b].T, axis=0, keepdims=True)
        theirs = jnp.sum(own_sums[b], axis=0, keepdims=True)
        potential_out[pl.ds(b, 1), :] = mine + theirs
        return carry

    lax.fori_loop(0, BOX, finish, 0)

    @pl.when(level < levels - 1)
    def _():
        back_copy.wait_recv()
        potential_out[...] = potential_out[...] + back_in[...]
        halo_copy.wait_send()

    @pl.when(level > 0)
    def _():
        back_copy.wait_send()

    potential_out[...] = jnp.where(occupied, potential_out[...], 0.0)
    loads["ops"].wait()

    in_group = (GROUP - 1 - zone % GROUP) * (1 - moved)

    @pl.when(in_group > 0)
    def _():
        pl.semaphore_wait(ready.at[group], in_group)
        over(zone + 1, zone + 1 + in_group, send)

    @pl.when(extra == 1)
    def _():
        pl.semaphore_wait(ready.at[GROUP], 1)
        send(0)

    for g in (1, 2, 3, 7, 6, 5, 4):

        @pl.when(group + moved < g)
        def _():
            pl.semaphore_wait(ready.at[g], GROUP)
            over(GROUP * g, GROUP * g + GROUP, send)

    over(0, zone, collect)
    over(zone + 1, ZONES, collect)
    columns = table[...].reshape(S, HALF).T
    for b in range(BOX):
        gathered[:, b, :] = gathered[:, b, :] + dot(columns, named[b])

    def translate(s, total):
        for w in range(11):
            p = s * 11 + w
            total = total + dot(gathered[p].astype(BF16), ops[p])
        return total

    far = lax.fori_loop(0, P2 // 11, translate, jnp.zeros((BOX, P2), F32), unroll=True)
    local_out[...] = local_out[...] + far
    whole = chosen.at[pl.ds(1, ZONES - 1)]
    pltpu.make_async_copy(whole, whole, slot_send).wait()


def per_device(
    multipoles,
    operators,
    parent_locals,
    shifts,
    send_slots,
    lists,
    positions,
    charges,
    counts,
    near_lists,
):
    arguments = (
        multipoles,
        operators.transpose(1, 0, 2),
        parent_locals,
        shifts.transpose(1, 0, 2),
        send_slots.transpose(0, 2, 1),
        lists,
        positions.transpose(1, 0, 2),
        charges,
        counts,
        near_lists,
    )
    vmem = pl.BlockSpec(memory_space=pltpu.VMEM)
    specs = [pl.BlockSpec(memory_space=pltpu.HBM)] * 10
    return pl.pallas_call(
        kernel,
        out_shape=(
            pltpu.VMEM((BOX, P2), F32),
            pltpu.VMEM((BOX, S), F32),
        ),
        in_specs=specs,
        out_specs=(vmem, vmem),
        scratch_shapes=[pltpu.VMEM(x.shape, x.dtype) for x in arguments]
        + [
            pltpu.VMEM((4, BOX, S), F32),
            pltpu.VMEM((4, BOX, S), F32),
            pltpu.VMEM((BOX, S), F32),
            pltpu.VMEM((BOX, S), F32),
            pltpu.VMEM((ZONES, 4, HALF), BF16),
            pltpu.VMEM((ZONES, 4, HALF), BF16),
            pltpu.VMEM((BOX, FEATURES, S), F32),
            pltpu.VMEM((BOX, FEATURES, S), BF16),
            pltpu.VMEM((BOX, FEATURES, S), BF16),
            pltpu.VMEM((BOX, S, FEATURES), BF16),
            pltpu.VMEM((BOX, S, HALF), F32),
            pltpu.VMEM((BOX, WINDOW, HALF), F32),
            pltpu.VMEM((BOX, S, HALF), F32),
            pltpu.VMEM((BOX, 8, S), F32),
            pltpu.VMEM((BOX, 8, S), F32),
            pltpu.VMEM((BOX, S, OFFSETS), BF16),
            pltpu.VMEM((HALF, BOX, OFFSETS), F32),
            pltpu.VMEM((2, HALF, HALF), F32),
            pltpu.SemaphoreType.DMA((10,)),
            pltpu.SemaphoreType.DMA((2,)),
            pltpu.SemaphoreType.DMA((2,)),
            pltpu.SemaphoreType.DMA,
            pltpu.SemaphoreType.DMA((ZONES,)),
            pltpu.SemaphoreType.REGULAR((GROUP + 1,)),
        ],
        compiler_params=pltpu.CompilerParams(
            collective_id=0, has_side_effects=True, vmem_limit_bytes=60 * 2**20
        ),
    )(*arguments)


def solution(mesh):
    placed = (
        P(("zone", "level"), None),
        P(),
        P(("zone", "level"), None),
        P(),
        P(("zone", "level"), None, None),
        P(("zone", "level"), None),
        P(("zone", "level"), None, None),
        P(("zone", "level"), None),
        P(("zone", "level")),
        P(("zone", "level"), None),
    )
    return jax.shard_map(
        per_device,
        mesh=mesh,
        in_specs=placed,
        out_specs=(P(("zone", "level"), None), P(("zone", "level"), None)),
        check_vma=False,
    )
```

```python
import jax
import jax.numpy as jnp
from jax import lax
from jax.experimental import pallas as pl
from jax.experimental.pallas import tpu as pltpu
from jax.sharding import PartitionSpec as P

soften = 0.0025
BOX = 16
S = 256
HALF = 128
FEATURES = 32
NEAR = 27
WINDOW = 48
OFFSETS = 189
P2 = 121
GROUP = 8
ZONES = 64
MOVED = 16
FAR = 32
WORK_FIRST = 48
MESH = pl.DeviceIdType.MESH
F32 = jnp.float32
BF16 = jnp.bfloat16


def iota(shape, dim):
    return lax.broadcasted_iota(jnp.int32, shape, dim)


def flag(mask, kind=BF16):
    return jnp.where(mask, 1.0, 0.0).astype(kind)


def dot(a, b):
    return jnp.dot(a, b, preferred_element_type=F32)


def dot_t(a, b):
    return lax.dot_general(a, b, (((1,), (1,)), ((), ())), preferred_element_type=F32)


def code(across, along):
    return across % 2 + 4 * (across // 2) + 2 * (along % 2) + 8 * (along // 2)


def split(x):
    high = x.astype(BF16).astype(F32)
    rest = x - high
    middle = rest.astype(BF16).astype(F32)
    return high, middle, rest - middle


def write_features(ref, coordinates, target):
    parts = [split(u) for u in coordinates]
    norm = coordinates[0] * coordinates[0]
    for u in coordinates[1:]:
        norm = norm + u * u
    ones = jnp.ones_like(norm)
    zeros = jnp.zeros_like(norm)
    rows = []
    for high, middle, low in parts:
        if target:
            rows += [-2.0 * r for r in (high, high, middle, middle, high, low)]
        else:
            rows += [high, middle, high, middle, low, high]
    if target:
        rows += list(split(norm)) + [ones] * 3
    else:
        rows += [ones] * 3 + list(split(norm + soften))
    rows += [zeros] * (FEATURES - len(rows))
    for k, row in enumerate(rows):
        ref[:, k, :] = row


def over(low, high, body):
    def one(peer, carry):
        body(peer)
        return carry

    lax.fori_loop(low, high, one, 0)


def kernel(
    multipoles_hbm,
    operators_hbm,
    parents_hbm,
    shifts_hbm,
    slots_hbm,
    lists_hbm,
    positions_hbm,
    charges_hbm,
    counts_hbm,
    near_hbm,
    local_out,
    potential_out,
    multipoles,
    ops,
    parents,
    shifts,
    slots,
    lists,
    positions,
    charges,
    counts,
    near,
    halo_out,
    halo_in,
    back_out,
    back_in,
    chosen,
    table,
    features,
    sources,
    below,
    targets,
    charge_columns,
    present,
    sums,
    own_sums,
    below_sums,
    named,
    gathered,
    parent_columns,
    load_sem,
    halo_sem,
    back_sem,
    slot_send,
    slot_recv,
    ready,
    inbound,
    outbound,
    inbound_recv,
    outbound_recv,
    relay_send,
):
    zone = lax.axis_index("zone")
    level = lax.axis_index("level")
    levels = lax.axis_size("level")
    group = zone // GROUP
    top = level // (levels - 1)
    first = (levels - 1 - level) // (levels - 1)
    origin = (ZONES - 1 - zone) // (ZONES - 1)
    moved = first * origin
    extra = first * (1 - origin) * ((ZONES + MOVED - 1 - zone) // ZONES)
    far = first * ((group + 4) // GROUP - (group + 3) // GROUP)
    relay = first * ((zone + ZONES - 1) // ZONES - (zone + ZONES - 2) // ZONES)
    before = (extra + moved + far, zone + MOVED * moved)
    after = (zone + 1 + (MOVED - 1) * moved, ZONES)

    loads = {}
    for k, (name, source, held) in enumerate(
        (
            ("multipoles", multipoles_hbm, multipoles),
            ("slots", slots_hbm, slots),
            ("counts", counts_hbm, counts),
            ("positions", positions_hbm, positions),
            ("charges", charges_hbm, charges),
            ("near", near_hbm, near),
            ("lists", lists_hbm, lists),
            ("parents", parents_hbm, parents),
            ("shifts", shifts_hbm, shifts),
            ("ops", operators_hbm, ops),
        )
    ):
        loads[name] = pltpu.make_async_copy(source, held, load_sem.at[k])

    loads["slots"].start()
    loads["multipoles"].start()

    barrier = pltpu.get_barrier_semaphore()

    def signal(semaphore, zone_to, level_to):
        pl.semaphore_signal(
            semaphore, inc=1, device_id=(zone_to, level_to), device_id_type=MESH
        )

    def tell(low, high):
        over(0, high - low, lambda k: signal(barrier, high - 1 - k, level))

    @pl.when(moved == 1)
    def _():
        tell(FAR + GROUP, ZONES)

    tell(after[0], ZONES - FAR * moved)

    @pl.when(level > 0)
    def _():
        signal(barrier, zone, level - 1)

    @pl.when(extra == 1)
    def _():
        signal(barrier, 0, level)

    for name in ("counts", "positions", "charges", "near", "lists", "parents", "shifts", "ops"):
        loads[name].start()

    def slot_copy(source, place, peer):
        return pltpu.make_async_remote_copy(
            src_ref=chosen.at[source],
            dst_ref=table.at[place],
            send_sem=slot_send,
            recv_sem=slot_recv,
            device_id=(peer, level),
            device_id_type=MESH,
        )

    def send(peer):
        slot_copy(peer, zone, peer).start()

    def greet(peer):
        signal(ready.at[group + GROUP * moved], peer, level)

    def send_early(peer):
        send(peer)
        greet(peer)

    def to_relay(source, target, receive):
        return pltpu.make_async_remote_copy(
            src_ref=source,
            dst_ref=target,
            send_sem=slot_send,
            recv_sem=receive,
            device_id=(1, level),
            device_id_type=MESH,
        )

    inward = to_relay(chosen.at[0], inbound.at[zone % GROUP], inbound_recv.at[zone % GROUP])
    outward = to_relay(chosen.at[pl.ds(FAR, GROUP)], outbound, outbound_recv)

    def pass_in():
        return pltpu.make_async_remote_copy(
            src_ref=inbound,
            dst_ref=table.at[pl.ds(FAR, GROUP)],
            send_sem=relay_send,
            recv_sem=slot_recv,
            device_id=(0, level),
            device_id_type=MESH,
        )

    def pass_out(k):
        return pltpu.make_async_remote_copy(
            src_ref=outbound.at[k],
            dst_ref=table.at[0],
            send_sem=relay_send,
            recv_sem=slot_recv,
            device_id=(FAR + k, level),
            device_id_type=MESH,
        )

    loads["multipoles"].wait()
    loads["slots"].wait()
    own = jnp.concatenate([multipoles[...], jnp.zeros((BOX, HALF - P2), BF16)], axis=1)
    reader = iota((S, ZONES), 0) // 4
    slot_rows = dot_t(flag(reader == iota((S, ZONES), 1)), slots[0].astype(F32).astype(BF16))
    mine = iota((S, 4), 0) % 4 == iota((S, 4), 1)
    picked = jnp.where(mine, slot_rows, 0.0).astype(BF16)
    box_of = dot(picked, jnp.ones((4, BOX), BF16))
    one_hot = flag(box_of == iota((S, BOX), 1).astype(F32))
    chosen[...] = dot(one_hot, own).reshape(ZONES, 4, HALF).astype(BF16)

    for name in ("counts", "positions", "charges"):
        loads[name].wait()
    diagonal = iota((BOX, BOX), 0) == iota((BOX, BOX), 1)
    count_row = counts[...].reshape(1, BOX).astype(F32)
    count_column = jnp.sum(jnp.where(diagonal, count_row, 0.0), axis=1, keepdims=True)
    occupied = iota((BOX, S), 1).astype(F32) < count_column
    for c in range(3):
        x = positions[c]
        halo_out[c] = jnp.where(occupied, x, x[:, 0:1])
    halo_out[3] = jnp.where(occupied, charges[...], 0.0)

    halo_copy = pltpu.make_async_remote_copy(
        src_ref=halo_out,
        dst_ref=halo_in,
        send_sem=halo_sem.at[0],
        recv_sem=halo_sem.at[1],
        device_id=(zone, (level + 1) % levels),
        device_id_type=MESH,
    )
    back_copy = pltpu.make_async_remote_copy(
        src_ref=back_out,
        dst_ref=back_in,
        send_sem=back_sem.at[0],
        recv_sem=back_sem.at[1],
        device_id=(zone, (level + levels - 1) % levels),
        device_id_type=MESH,
    )

    middle = [jnp.sum(halo_out[c, :, 0:1], axis=0, keepdims=True) * (1.0 / BOX) for c in range(3)]

    def block(b, n, shift, side, charge, other):
        y = lax.rsqrt(dot(targets[b], side[n]))
        if other is None:
            y = jnp.where(iota((S, S), 0) == iota((S, S), 1), 0.0, y)
        there = present[b, pl.ds(shift + n, 1), :]
        row = charge[3, pl.ds(n, 1), :]
        left, right = y[:, :HALF], y[:, HALF:]
        sums[b] = sums[b] + (left * (row[:, :HALF] * there) + right * (row[:, HALF:] * there))
        if other is not None:
            column = charge_columns[b]
            for half, part in ((0, left), (HALF, right)):
                total = (part * column).reshape(S // 8, 8, HALF).sum(0)
                other[n, :, half : half + HALF] = (
                    other[n, :, half : half + HALF] + total * there
                )

    def own_block(b, n):
        block(b, n, BOX, sources, halo_out, own_sums)

    def own_pairs(s, carry):
        for w in range(4):
            own_block(code(s, w), code(s + 1, w))
            own_block(code(w, s), code(w, s + 1))
        for w in range(3):
            own_block(code(s, w), code(s + 1, w + 1))
            own_block(code(s + 1, w), code(s, w + 1))
        return carry

    def self_pairs(s, carry):
        for w in range(4):
            block(4 * s + w, 4 * s + w, BOX, sources, halo_out, None)
        return carry

    def below_pairs(t, carry):
        x = (t + 1) // 3
        x_next = t - 2 * x
        for w in range(10):
            y = (w + 1) // 3
            y_next = w - 2 * y
            block(code(x, y), code(x_next, y_next), 0, below, halo_in, below_sums)
        return carry

    def prepare_and_pair():
        offsets = [halo_out[c] - middle[c] for c in range(3)]
        identity = flag(iota((S, S), 0) == iota((S, S), 1))
        write_features(features, offsets, True)

        def prepare(b, carry):
            targets[b] = dot_t(identity, features[b].astype(BF16)).astype(BF16)
            row = jnp.broadcast_to(halo_out[3, pl.ds(b, 1), :], (HALF, S))
            charge_columns[b] = row.T
            sums[b] = jnp.zeros((S, HALF), F32)
            return carry

        lax.fori_loop(0, BOX, prepare, 0)
        write_features(features, offsets, False)
        sources[...] = features[...].astype(BF16)
        own_sums[...] = jnp.zeros_like(own_sums)
        below_sums[...] = jnp.zeros_like(below_sums)
        loads["near"].wait()
        hits = flag(near[...][:, None, :] == iota((BOX, WINDOW, NEAR), 1))
        present[...] = dot(
            hits.reshape(BOX * WINDOW, NEAR), jnp.ones((NEAR, HALF), BF16)
        ).reshape(BOX, WINDOW, HALF)

        lax.fori_loop(0, 3, own_pairs, 0)

    def name_members():
        loads["lists"].wait()
        own_columns = own.T
        entry = BOX + iota((S, OFFSETS), 0)
        for b in range(BOX):
            row = lists[b : b + 1, :]
            named[b] = flag(entry == row)
            gathered[:, b, :] = dot(own_columns, flag(iota((BOX, OFFSETS), 0) == row))

        loads["parents"].wait()
        loads["shifts"].wait()
        for g in range(2):
            row = jnp.concatenate([parents[g : g + 1, :], jnp.zeros((1, HALF - P2), F32)], axis=1)
            parent_columns[g] = jnp.broadcast_to(row, (HALF, HALF)).T
        for g in range(2):
            total = jnp.zeros((8, P2), F32)
            for p in range(P2):
                total = total + parent_columns[g, p : p + 1, :P2] * shifts[p]
            local_out[8 * g : 8 * g + 8, :] = total

    def send_first():
        count_before = before[1] - before[0]

        @pl.when(count_before + 1 - top > 0)
        def _():
            pl.semaphore_wait(barrier, count_before + 1 - top)

        @pl.when(here == 1)
        def _():
            over(*before, send_early)

        @pl.when(here == 0)
        def _():
            over(*before, greet)
            over(*before, send)

        @pl.when(far == 1)
        def _():
            inward.start()

        @pl.when(moved == 1)
        def _():
            outward.start()

        table[zone] = chosen[zone]

        @pl.when(level < levels - 1)
        def _():
            halo_copy.start()

    here = 1 - (zone + ZONES - WORK_FIRST) // ZONES

    def phase(k, carry):
        @pl.when(k == here)
        def _():
            prepare_and_pair()

        @pl.when(k == 1 - here)
        def _():
            send_first()

        return carry

    lax.fori_loop(0, 2, phase, 0)
    lax.fori_loop(0, 4, self_pairs, 0)
    name_members()

    @pl.when(level > 0)
    def _():
        halo_copy.wait_recv()
        write_features(features, [halo_in[c] - middle[c] for c in range(3)], False)
        below[...] = features[...].astype(BF16)
        lax.fori_loop(0, 10, below_pairs, 0)
        back_out[...] = jnp.sum(below_sums[...], axis=1)
        back_copy.start()

    def finish(b, carry):
        mine = jnp.sum(sums[b].T, axis=0, keepdims=True)
        theirs = jnp.sum(own_sums[b], axis=0, keepdims=True)
        potential_out[pl.ds(b, 1), :] = mine + theirs
        return carry

    lax.fori_loop(0, BOX, finish, 0)

    @pl.when(level < levels - 1)
    def _():
        back_copy.wait_recv()
        potential_out[...] = potential_out[...] + back_in[...]
        halo_copy.wait_send()

    @pl.when(level > 0)
    def _():
        back_copy.wait_send()

    potential_out[...] = jnp.where(occupied, potential_out[...], 0.0)
    loads["ops"].wait()

    in_group = (GROUP - 1 - zone % GROUP) * (1 - moved)

    @pl.when(in_group > 0)
    def _():
        pl.semaphore_wait(ready.at[group], in_group)
        over(zone + 1, zone + 1 + in_group, send)

    @pl.when(extra == 1)
    def _():
        pl.semaphore_wait(ready.at[GROUP], 1)
        send(0)

    for g in range(1, GROUP):

        @pl.when(group + (4 if g == 4 else 1) * moved < g)
        def _():
            pl.semaphore_wait(ready.at[g], GROUP)
            over(GROUP * g, GROUP * g + GROUP, send)

    @pl.when(relay == 1)
    def _():
        outward.wait_recv()

        def pass_one(k, carry):
            pass_out(k).start()
            return carry

        lax.fori_loop(0, GROUP, pass_one, 0)
        for k in range(GROUP):
            to_relay(chosen.at[0], inbound.at[k], inbound_recv.at[k]).wait_recv()
        pass_in().start()

    others = table.at[pl.ds(1, ZONES - 1)]
    pltpu.make_async_copy(others, others, slot_recv).wait()
    columns = table[...].reshape(S, HALF).T
    for b in range(BOX):
        gathered[:, b, :] = gathered[:, b, :] + dot(columns, named[b])

    def translate(s, total):
        for w in range(11):
            p = s * 11 + w
            total = total + dot(gathered[p].astype(BF16), ops[p])
        return total

    far = lax.fori_loop(0, P2 // 11, translate, jnp.zeros((BOX, P2), F32), unroll=True)
    local_out[...] = local_out[...] + far
    whole = chosen.at[pl.ds(1, ZONES - 1)]
    pltpu.make_async_copy(whole, whole, slot_send).wait()

    @pl.when(relay == 1)
    def _():
        passed = chosen.at[pl.ds(0, 2 * GROUP)]
        pltpu.make_async_copy(passed, passed, relay_send).wait()


def per_device(
    multipoles,
    operators,
    parent_locals,
    shifts,
    send_slots,
    lists,
    positions,
    charges,
    counts,
    near_lists,
):
    arguments = (
        multipoles,
        operators.transpose(1, 0, 2),
        parent_locals,
        shifts.transpose(1, 0, 2),
        send_slots.transpose(0, 2, 1),
        lists,
        positions.transpose(1, 0, 2),
        charges,
        counts,
        near_lists,
    )
    vmem = pl.BlockSpec(memory_space=pltpu.VMEM)
    specs = [pl.BlockSpec(memory_space=pltpu.HBM)] * 10
    return pl.pallas_call(
        kernel,
        out_shape=(
            pltpu.VMEM((BOX, P2), F32),
            pltpu.VMEM((BOX, S), F32),
        ),
        in_specs=specs,
        out_specs=(vmem, vmem),
        scratch_shapes=[pltpu.VMEM(x.shape, x.dtype) for x in arguments]
        + [
            pltpu.VMEM((4, BOX, S), F32),
            pltpu.VMEM((4, BOX, S), F32),
            pltpu.VMEM((BOX, S), F32),
            pltpu.VMEM((BOX, S), F32),
            pltpu.VMEM((ZONES, 4, HALF), BF16),
            pltpu.VMEM((ZONES, 4, HALF), BF16),
            pltpu.VMEM((BOX, FEATURES, S), F32),
            pltpu.VMEM((BOX, FEATURES, S), BF16),
            pltpu.VMEM((BOX, FEATURES, S), BF16),
            pltpu.VMEM((BOX, S, FEATURES), BF16),
            pltpu.VMEM((BOX, S, HALF), F32),
            pltpu.VMEM((BOX, WINDOW, HALF), F32),
            pltpu.VMEM((BOX, S, HALF), F32),
            pltpu.VMEM((BOX, 8, S), F32),
            pltpu.VMEM((BOX, 8, S), F32),
            pltpu.VMEM((BOX, S, OFFSETS), BF16),
            pltpu.VMEM((HALF, BOX, OFFSETS), F32),
            pltpu.VMEM((2, HALF, HALF), F32),
            pltpu.SemaphoreType.DMA((10,)),
            pltpu.SemaphoreType.DMA((2,)),
            pltpu.SemaphoreType.DMA((2,)),
            pltpu.SemaphoreType.DMA,
            pltpu.SemaphoreType.DMA,
            pltpu.SemaphoreType.REGULAR((GROUP + 1,)),
            pltpu.VMEM((GROUP, 4, HALF), BF16),
            pltpu.VMEM((GROUP, 4, HALF), BF16),
            pltpu.SemaphoreType.DMA((GROUP,)),
            pltpu.SemaphoreType.DMA,
            pltpu.SemaphoreType.DMA,
        ],
        compiler_params=pltpu.CompilerParams(
            collective_id=0, has_side_effects=True, vmem_limit_bytes=60 * 2**20
        ),
    )(*arguments)


def solution(mesh):
    placed = (
        P(("zone", "level"), None),
        P(),
        P(("zone", "level"), None),
        P(),
        P(("zone", "level"), None, None),
        P(("zone", "level"), None),
        P(("zone", "level"), None, None),
        P(("zone", "level"), None),
        P(("zone", "level")),
        P(("zone", "level"), None),
    )
    return jax.shard_map(
        per_device,
        mesh=mesh,
        in_specs=placed,
        out_specs=(P(("zone", "level"), None), P(("zone", "level"), None)),
        check_vma=False,
    )
```

```python
import jax
import jax.numpy as jnp
from jax import lax
from jax.experimental import pallas as pl
from jax.experimental.pallas import tpu as pltpu
from jax.sharding import PartitionSpec as P

soften = 0.0025
BOX = 16
S = 256
HALF = 128
FEATURES = 32
NEAR = 27
WINDOW = 48
OFFSETS = 189
P2 = 121
GROUP = 8
ZONES = 64
MOVED = 16
FAR = 32
LODGED = 24
LAST = 56
WORK_FIRST = 48
MESH = pl.DeviceIdType.MESH
F32 = jnp.float32
BF16 = jnp.bfloat16


def iota(shape, dim):
    return lax.broadcasted_iota(jnp.int32, shape, dim)


def flag(mask, kind=BF16):
    return jnp.where(mask, 1.0, 0.0).astype(kind)


def dot(a, b):
    return jnp.dot(a, b, preferred_element_type=F32)


def dot_t(a, b):
    return lax.dot_general(a, b, (((1,), (1,)), ((), ())), preferred_element_type=F32)


def code(across, along):
    return across % 2 + 4 * (across // 2) + 2 * (along % 2) + 8 * (along // 2)


def split(x):
    high = x.astype(BF16).astype(F32)
    rest = x - high
    middle = rest.astype(BF16).astype(F32)
    return high, middle, rest - middle


def write_features(ref, coordinates, target):
    parts = [split(u) for u in coordinates]
    norm = coordinates[0] * coordinates[0]
    for u in coordinates[1:]:
        norm = norm + u * u
    ones = jnp.ones_like(norm)
    zeros = jnp.zeros_like(norm)
    rows = []
    for high, middle, low in parts:
        if target:
            rows += [-2.0 * r for r in (high, high, middle, middle, high, low)]
        else:
            rows += [high, middle, high, middle, low, high]
    if target:
        rows += list(split(norm)) + [ones] * 3
    else:
        rows += [ones] * 3 + list(split(norm + soften))
    rows += [zeros] * (FEATURES - len(rows))
    for k, row in enumerate(rows):
        ref[:, k, :] = row


def over(low, high, body):
    def one(peer, carry):
        body(peer)
        return carry

    lax.fori_loop(low, high, one, 0)


def kernel(
    multipoles_hbm,
    operators_hbm,
    parents_hbm,
    shifts_hbm,
    slots_hbm,
    lists_hbm,
    positions_hbm,
    charges_hbm,
    counts_hbm,
    near_hbm,
    local_out,
    potential_out,
    multipoles,
    ops,
    parents,
    shifts,
    slots,
    lists,
    positions,
    charges,
    counts,
    near,
    halo_out,
    halo_in,
    back_out,
    back_in,
    chosen,
    table,
    features,
    sources,
    below,
    targets,
    charge_columns,
    present,
    sums,
    own_sums,
    below_sums,
    named,
    gathered,
    parent_columns,
    load_sem,
    halo_sem,
    back_sem,
    slot_send,
    slot_recv,
    ready,
    inbound,
    outbound,
    inbound_recv,
    outbound_recv,
    relay_send,
    held_rows,
    held_recv,
    held_send,
):
    zone = lax.axis_index("zone")
    level = lax.axis_index("level")
    levels = lax.axis_size("level")
    group = zone // GROUP
    top = level // (levels - 1)
    first = (levels - 1 - level) // (levels - 1)
    origin = (ZONES - 1 - zone) // (ZONES - 1)
    moved = first * origin
    extra = first * (1 - origin) * ((ZONES + MOVED - 1 - zone) // ZONES)
    far = first * ((group + 4) // GROUP - (group + 3) // GROUP)
    relay = first * ((zone + ZONES - 1) // ZONES - (zone + ZONES - 2) // ZONES)
    lodger = (group + 5) // GROUP - (group + 4) // GROUP
    host = (GROUP - 1 - group) // (GROUP - 1)
    before = (extra + moved + far, zone + MOVED * moved)
    after = (zone + 1 + (MOVED - 1) * moved, ZONES)

    loads = {}
    for k, (name, source, held) in enumerate(
        (
            ("multipoles", multipoles_hbm, multipoles),
            ("slots", slots_hbm, slots),
            ("counts", counts_hbm, counts),
            ("positions", positions_hbm, positions),
            ("charges", charges_hbm, charges),
            ("near", near_hbm, near),
            ("lists", lists_hbm, lists),
            ("parents", parents_hbm, parents),
            ("shifts", shifts_hbm, shifts),
            ("ops", operators_hbm, ops),
        )
    ):
        loads[name] = pltpu.make_async_copy(source, held, load_sem.at[k])

    loads["slots"].start()
    loads["multipoles"].start()

    barrier = pltpu.get_barrier_semaphore()

    def signal(semaphore, zone_to, level_to):
        pl.semaphore_signal(
            semaphore, inc=1, device_id=(zone_to, level_to), device_id_type=MESH
        )

    def tell(low, high):
        over(0, high - low, lambda k: signal(barrier, high - 1 - k, level))

    @pl.when(moved == 1)
    def _():
        tell(FAR + GROUP, ZONES)

    tell(after[0], ZONES - FAR * moved)

    @pl.when(level > 0)
    def _():
        signal(barrier, zone, level - 1)

    @pl.when(extra == 1)
    def _():
        signal(barrier, 0, level)

    for name in ("counts", "positions", "charges", "near", "lists", "parents", "shifts", "ops"):
        loads[name].start()

    def slot_copy(source, place, peer):
        return pltpu.make_async_remote_copy(
            src_ref=chosen.at[source],
            dst_ref=table.at[place],
            send_sem=slot_send,
            recv_sem=slot_recv,
            device_id=(peer, level),
            device_id_type=MESH,
        )

    def send(peer):
        slot_copy(peer, zone, peer).start()

    def greet(peer):
        signal(ready.at[group + GROUP * moved], peer, level)

    def send_early(peer):
        send(peer)
        greet(peer)

    def to_relay(source, target, receive):
        return pltpu.make_async_remote_copy(
            src_ref=source,
            dst_ref=target,
            send_sem=slot_send,
            recv_sem=receive,
            device_id=(1, level),
            device_id_type=MESH,
        )

    inward = to_relay(chosen.at[0], inbound.at[zone % GROUP], inbound_recv.at[zone % GROUP])
    outward = to_relay(chosen.at[pl.ds(FAR, GROUP)], outbound, outbound_recv)

    lodge = pltpu.make_async_remote_copy(
        src_ref=chosen.at[pl.ds(LAST, GROUP)],
        dst_ref=held_rows,
        send_sem=slot_send,
        recv_sem=held_recv,
        device_id=(zone % GROUP, level),
        device_id_type=MESH,
    )

    def pass_held(k):
        return pltpu.make_async_remote_copy(
            src_ref=held_rows.at[k],
            dst_ref=table.at[LODGED + zone % GROUP],
            send_sem=held_send,
            recv_sem=slot_recv,
            device_id=(LAST + k, level),
            device_id_type=MESH,
        )

    def pass_in():
        return pltpu.make_async_remote_copy(
            src_ref=inbound,
            dst_ref=table.at[pl.ds(FAR, GROUP)],
            send_sem=relay_send,
            recv_sem=slot_recv,
            device_id=(0, level),
            device_id_type=MESH,
        )

    def pass_out(k):
        return pltpu.make_async_remote_copy(
            src_ref=outbound.at[k],
            dst_ref=table.at[0],
            send_sem=relay_send,
            recv_sem=slot_recv,
            device_id=(FAR + k, level),
            device_id_type=MESH,
        )

    loads["multipoles"].wait()
    loads["slots"].wait()
    own = jnp.concatenate([multipoles[...], jnp.zeros((BOX, HALF - P2), BF16)], axis=1)
    reader = iota((S, ZONES), 0) // 4
    slot_rows = dot_t(flag(reader == iota((S, ZONES), 1)), slots[0].astype(F32).astype(BF16))
    mine = iota((S, 4), 0) % 4 == iota((S, 4), 1)
    picked = jnp.where(mine, slot_rows, 0.0).astype(BF16)
    box_of = dot(picked, jnp.ones((4, BOX), BF16))
    one_hot = flag(box_of == iota((S, BOX), 1).astype(F32))
    chosen[...] = dot(one_hot, own).reshape(ZONES, 4, HALF).astype(BF16)

    for name in ("counts", "positions", "charges"):
        loads[name].wait()
    diagonal = iota((BOX, BOX), 0) == iota((BOX, BOX), 1)
    count_row = counts[...].reshape(1, BOX).astype(F32)
    count_column = jnp.sum(jnp.where(diagonal, count_row, 0.0), axis=1, keepdims=True)
    occupied = iota((BOX, S), 1).astype(F32) < count_column
    for c in range(3):
        x = positions[c]
        halo_out[c] = jnp.where(occupied, x, x[:, 0:1])
    halo_out[3] = jnp.where(occupied, charges[...], 0.0)

    halo_copy = pltpu.make_async_remote_copy(
        src_ref=halo_out,
        dst_ref=halo_in,
        send_sem=halo_sem.at[0],
        recv_sem=halo_sem.at[1],
        device_id=(zone, (level + 1) % levels),
        device_id_type=MESH,
    )
    back_copy = pltpu.make_async_remote_copy(
        src_ref=back_out,
        dst_ref=back_in,
        send_sem=back_sem.at[0],
        recv_sem=back_sem.at[1],
        device_id=(zone, (level + levels - 1) % levels),
        device_id_type=MESH,
    )

    middle = [jnp.sum(halo_out[c, :, 0:1], axis=0, keepdims=True) * (1.0 / BOX) for c in range(3)]

    def block(b, n, shift, side, charge, other):
        y = lax.rsqrt(dot(targets[b], side[n]))
        if other is None:
            y = jnp.where(iota((S, S), 0) == iota((S, S), 1), 0.0, y)
        there = present[b, pl.ds(shift + n, 1), :]
        row = charge[3, pl.ds(n, 1), :]
        left, right = y[:, :HALF], y[:, HALF:]
        sums[b] = sums[b] + (left * (row[:, :HALF] * there) + right * (row[:, HALF:] * there))
        if other is not None:
            column = charge_columns[b]
            for half, part in ((0, left), (HALF, right)):
                total = (part * column).reshape(S // 8, 8, HALF).sum(0)
                other[n, :, half : half + HALF] = (
                    other[n, :, half : half + HALF] + total * there
                )

    def own_block(b, n):
        block(b, n, BOX, sources, halo_out, own_sums)

    def own_pairs(s, carry):
        for w in range(4):
            own_block(code(s, w), code(s + 1, w))
            own_block(code(w, s), code(w, s + 1))
        for w in range(3):
            own_block(code(s, w), code(s + 1, w + 1))
            own_block(code(s + 1, w), code(s, w + 1))
        return carry

    def self_pairs(s, carry):
        for w in range(4):
            block(4 * s + w, 4 * s + w, BOX, sources, halo_out, None)
        return carry

    def below_pairs(t, carry):
        x = (t + 1) // 3
        x_next = t - 2 * x
        for w in range(10):
            y = (w + 1) // 3
            y_next = w - 2 * y
            block(code(x, y), code(x_next, y_next), 0, below, halo_in, below_sums)
        return carry

    def prepare_and_pair():
        offsets = [halo_out[c] - middle[c] for c in range(3)]
        identity = flag(iota((S, S), 0) == iota((S, S), 1))
        write_features(features, offsets, True)

        def prepare(b, carry):
            targets[b] = dot_t(identity, features[b].astype(BF16)).astype(BF16)
            row = jnp.broadcast_to(halo_out[3, pl.ds(b, 1), :], (HALF, S))
            charge_columns[b] = row.T
            sums[b] = jnp.zeros((S, HALF), F32)
            return carry

        lax.fori_loop(0, BOX, prepare, 0)
        write_features(features, offsets, False)
        sources[...] = features[...].astype(BF16)
        own_sums[...] = jnp.zeros_like(own_sums)
        below_sums[...] = jnp.zeros_like(below_sums)
        loads["near"].wait()
        hits = flag(near[...][:, None, :] == iota((BOX, WINDOW, NEAR), 1))
        present[...] = dot(
            hits.reshape(BOX * WINDOW, NEAR), jnp.ones((NEAR, HALF), BF16)
        ).reshape(BOX, WINDOW, HALF)

        lax.fori_loop(0, 3, own_pairs, 0)

    def name_members():
        loads["lists"].wait()
        own_columns = own.T
        entry = BOX + iota((S, OFFSETS), 0)
        for b in range(BOX):
            row = lists[b : b + 1, :]
            named[b] = flag(entry == row)
            gathered[:, b, :] = dot(own_columns, flag(iota((BOX, OFFSETS), 0) == row))

        loads["parents"].wait()
        loads["shifts"].wait()
        for g in range(2):
            row = jnp.concatenate([parents[g : g + 1, :], jnp.zeros((1, HALF - P2), F32)], axis=1)
            parent_columns[g] = jnp.broadcast_to(row, (HALF, HALF)).T
        for g in range(2):
            total = jnp.zeros((8, P2), F32)
            for p in range(P2):
                total = total + parent_columns[g, p : p + 1, :P2] * shifts[p]
            local_out[8 * g : 8 * g + 8, :] = total

    def send_first():
        count_before = before[1] - before[0]

        @pl.when(count_before + 1 - top > 0)
        def _():
            pl.semaphore_wait(barrier, count_before + 1 - top)

        @pl.when(here == 1)
        def _():
            over(*before, send_early)

        @pl.when(here == 0)
        def _():
            over(*before, greet)
            over(*before, send)

        @pl.when(lodger == 1)
        def _():
            lodge.start()

        @pl.when(far == 1)
        def _():
            inward.start()

        @pl.when(moved == 1)
        def _():
            outward.start()

        table[zone] = chosen[zone]

        @pl.when(level < levels - 1)
        def _():
            halo_copy.start()

    here = 1 - (zone + ZONES - WORK_FIRST) // ZONES

    def phase(k, carry):
        @pl.when(k == here)
        def _():
            prepare_and_pair()

        @pl.when(k == 1 - here)
        def _():
            send_first()

        return carry

    lax.fori_loop(0, 2, phase, 0)
    lax.fori_loop(0, 4, self_pairs, 0)
    name_members()

    late = (zone + ZONES - FAR) // ZONES

    def answer_all():
        in_group = (GROUP - 1 - zone % GROUP) * (1 - moved)

        @pl.when(in_group > 0)
        def _():
            pl.semaphore_wait(ready.at[group], in_group)
            over(zone + 1, zone + 1 + in_group, send)

        @pl.when(extra == 1)
        def _():
            pl.semaphore_wait(ready.at[GROUP], 1)
            send(0)

        for g in range(1, GROUP):

            @pl.when(group + (4 if g == 4 else 1) * moved < g)
            def _():
                pl.semaphore_wait(ready.at[g], GROUP)
                skip = GROUP * lodger if g == GROUP - 1 else 0
                over(GROUP * g + skip, GROUP * g + GROUP, send)

    @pl.when(late == 1)
    def _():
        answer_all()

    @pl.when(level > 0)
    def _():
        halo_copy.wait_recv()
        write_features(features, [halo_in[c] - middle[c] for c in range(3)], False)
        below[...] = features[...].astype(BF16)
        lax.fori_loop(0, 10, below_pairs, 0)
        back_out[...] = jnp.sum(below_sums[...], axis=1)
        back_copy.start()

    def finish(b, carry):
        mine = jnp.sum(sums[b].T, axis=0, keepdims=True)
        theirs = jnp.sum(own_sums[b], axis=0, keepdims=True)
        potential_out[pl.ds(b, 1), :] = mine + theirs
        return carry

    lax.fori_loop(0, BOX, finish, 0)

    @pl.when(level < levels - 1)
    def _():
        back_copy.wait_recv()
        potential_out[...] = potential_out[...] + back_in[...]
        halo_copy.wait_send()

    @pl.when(level > 0)
    def _():
        back_copy.wait_send()

    potential_out[...] = jnp.where(occupied, potential_out[...], 0.0)
    loads["ops"].wait()

    @pl.when(late == 0)
    def _():
        answer_all()

    @pl.when(relay == 1)
    def _():
        outward.wait_recv()

        def pass_one(k, carry):
            pass_out(k).start()
            return carry

        lax.fori_loop(0, GROUP, pass_one, 0)
        for k in range(GROUP):
            to_relay(chosen.at[0], inbound.at[k], inbound_recv.at[k]).wait_recv()
        pass_in().start()

    @pl.when(host == 1)
    def _():
        lodge.wait_recv()

        def pass_one(k, carry):
            pass_held(k).start()
            return carry

        lax.fori_loop(0, GROUP, pass_one, 0)

    others = table.at[pl.ds(1, ZONES - 1)]
    pltpu.make_async_copy(others, others, slot_recv).wait()
    columns = table[...].reshape(S, HALF).T
    for b in range(BOX):
        gathered[:, b, :] = gathered[:, b, :] + dot(columns, named[b])

    def translate(s, total):
        for w in range(11):
            p = s * 11 + w
            total = total + dot(gathered[p].astype(BF16), ops[p])
        return total

    far = lax.fori_loop(0, P2 // 11, translate, jnp.zeros((BOX, P2), F32), unroll=True)
    local_out[...] = local_out[...] + far
    whole = chosen.at[pl.ds(1, ZONES - 1)]
    pltpu.make_async_copy(whole, whole, slot_send).wait()

    @pl.when(host == 1)
    def _():
        passed = chosen.at[pl.ds(0, GROUP)]
        pltpu.make_async_copy(passed, passed, held_send).wait()

    @pl.when(relay == 1)
    def _():
        passed = chosen.at[pl.ds(0, 2 * GROUP)]
        pltpu.make_async_copy(passed, passed, relay_send).wait()


def per_device(
    multipoles,
    operators,
    parent_locals,
    shifts,
    send_slots,
    lists,
    positions,
    charges,
    counts,
    near_lists,
):
    arguments = (
        multipoles,
        operators.transpose(1, 0, 2),
        parent_locals,
        shifts.transpose(1, 0, 2),
        send_slots.transpose(0, 2, 1),
        lists,
        positions.transpose(1, 0, 2),
        charges,
        counts,
        near_lists,
    )
    vmem = pl.BlockSpec(memory_space=pltpu.VMEM)
    specs = [pl.BlockSpec(memory_space=pltpu.HBM)] * 10
    return pl.pallas_call(
        kernel,
        out_shape=(
            pltpu.VMEM((BOX, P2), F32),
            pltpu.VMEM((BOX, S), F32),
        ),
        in_specs=specs,
        out_specs=(vmem, vmem),
        scratch_shapes=[pltpu.VMEM(x.shape, x.dtype) for x in arguments]
        + [
            pltpu.VMEM((4, BOX, S), F32),
            pltpu.VMEM((4, BOX, S), F32),
            pltpu.VMEM((BOX, S), F32),
            pltpu.VMEM((BOX, S), F32),
            pltpu.VMEM((ZONES, 4, HALF), BF16),
            pltpu.VMEM((ZONES, 4, HALF), BF16),
            pltpu.VMEM((BOX, FEATURES, S), F32),
            pltpu.VMEM((BOX, FEATURES, S), BF16),
            pltpu.VMEM((BOX, FEATURES, S), BF16),
            pltpu.VMEM((BOX, S, FEATURES), BF16),
            pltpu.VMEM((BOX, S, HALF), F32),
            pltpu.VMEM((BOX, WINDOW, HALF), F32),
            pltpu.VMEM((BOX, S, HALF), F32),
            pltpu.VMEM((BOX, 8, S), F32),
            pltpu.VMEM((BOX, 8, S), F32),
            pltpu.VMEM((BOX, S, OFFSETS), BF16),
            pltpu.VMEM((HALF, BOX, OFFSETS), F32),
            pltpu.VMEM((2, HALF, HALF), F32),
            pltpu.SemaphoreType.DMA((10,)),
            pltpu.SemaphoreType.DMA((2,)),
            pltpu.SemaphoreType.DMA((2,)),
            pltpu.SemaphoreType.DMA,
            pltpu.SemaphoreType.DMA,
            pltpu.SemaphoreType.REGULAR((GROUP + 1,)),
            pltpu.VMEM((GROUP, 4, HALF), BF16),
            pltpu.VMEM((GROUP, 4, HALF), BF16),
            pltpu.SemaphoreType.DMA((GROUP,)),
            pltpu.SemaphoreType.DMA,
            pltpu.SemaphoreType.DMA,
            pltpu.VMEM((GROUP, 4, HALF), BF16),
            pltpu.SemaphoreType.DMA,
            pltpu.SemaphoreType.DMA,
        ],
        compiler_params=pltpu.CompilerParams(
            collective_id=0, has_side_effects=True, vmem_limit_bytes=60 * 2**20
        ),
    )(*arguments)


def solution(mesh):
    placed = (
        P(("zone", "level"), None),
        P(),
        P(("zone", "level"), None),
        P(),
        P(("zone", "level"), None, None),
        P(("zone", "level"), None),
        P(("zone", "level"), None, None),
        P(("zone", "level"), None),
        P(("zone", "level")),
        P(("zone", "level"), None),
    )
    return jax.shard_map(
        per_device,
        mesh=mesh,
        in_specs=placed,
        out_specs=(P(("zone", "level"), None), P(("zone", "level"), None)),
        check_vma=False,
    )
```
